128 devices in a mesh: row: 16 (over z, y_hi, core), col: 8 (over x, y_lo).
Axes of the slice: x: 4, y: 4 (y_hi: 2, y_lo: 2; y = y_hi * 2 + y_lo), z: 4, core: 2. Of those that a mesh axis runs over, the one named last changes fastest.
Arguments:
- a_blocks: float32 [7168, 128, 128], P(('row', 'col')), may hold values from -0.1875 to 0.1875
- a_pick: int32 [16384], P(('row', 'col')), may hold values from 0 to 56, as said below
- a_place: int32 [7168], P(('row', 'col')), may hold values from 0 to 127, as said below
- b_blocks: float32 [7168, 128, 128], P(('row', 'col')), may hold values from -6 to 6
- b_pick: int32 [16384], P(('row', 'col')), may hold values from 0 to 56, as said below
- b_place: int32 [7168], P(('row', 'col')), may hold values from 0 to 127, as said below
- prod_a: int32 [4, 8192], P(None, ('row', 'col')), may hold values from 0 to 55
- prod_b: int32 [4, 8192], P(None, ('row', 'col')), may hold values from 0 to 55
- prod_c: int32 [4, 8192], P(None, ('row', 'col')), may hold values from 0 to 64, as said below
Outputs:
- c_blocks: float32 [8192, 128, 128], P(('row', 'col'))
The draws below stay inside these ranges and needn't reach their ends.
Inputs may be any that keep to these rules, and one draw needn't show every extreme that they name: `a_pick`: 56 marks an empty send slot; every source fills 56 slots, at most 1 to any one device, and exactly 1 to some device. `a_place`: each device's list names 56 distinct filled arrived slots. `b_pick`: 56 marks an empty send slot; every source fills 56 slots, at most 1 to any one device, and exactly 1 to some device. `b_place`: each device's list names 56 distinct filled arrived slots. `prod_c`: 64 marks an unused entry; in every step some device uses all 64 entries and every device uses a third of them or more.
All inputs are finite; a program needn't handle non-finite values.
Results may differ from the reference program's by a relative error of at most 0.0003.
Values sent between devices are 32-bit elements; how exact they have to be, the bound alone decides.
No kernel may reach another device: no remote copies, remote signals or barrier semaphores. Data moves between devices by JAX's collectives and lax.ppermute only.
A program may use at most 128 MiB of HBM per device.

```python
import jax
import jax.numpy as jnp
from jax import lax

BS = 128
PANEL = 56
CBLK = 64
PROD = 64
STEPS = 4
CAP = 1
NBLK = 7168
CTOT = 8192
N_ROW = 16
N_COL = 8
DEVICES = 128


def layout(key, salt):
    key = jax.random.fold_in(key, salt)
    keys = jax.random.split(key, 5)
    sigma = jax.random.permutation(keys[0], DEVICES).astype(jnp.int32)
    tau = jax.random.permutation(keys[1], DEVICES).astype(jnp.int32)
    sigma_inv = jnp.argsort(sigma).astype(jnp.int32)
    tau_inv = jnp.argsort(tau).astype(jnp.int32)
    others = jax.random.permutation(keys[2], DEVICES * CAP - CAP).astype(jnp.int32)
    mapped = others // (DEVICES - 1) * DEVICES + others % (DEVICES - 1) + 1
    offsets = jnp.concatenate([jnp.arange(CAP, dtype=jnp.int32) * DEVICES, mapped[:PANEL - CAP]])
    shifts = offsets % DEVICES
    ranks = offsets // DEVICES
    sources = jnp.arange(DEVICES, dtype=jnp.int32)
    targets = tau[(sigma[:, None] + shifts[None, :]) % DEVICES]
    orders = jax.vmap(lambda k: jax.random.permutation(k, PANEL))(jax.random.split(keys[3], DEVICES)).astype(jnp.int32)
    pick = jnp.full((DEVICES, DEVICES * CAP), PANEL, jnp.int32)
    pick = pick.at[jnp.broadcast_to(sources[:, None], (DEVICES, PANEL)), targets * CAP + ranks[None, :]].set(orders)
    senders = sigma_inv[(tau_inv[:, None] - shifts[None, :]) % DEVICES]
    entries = senders * CAP + ranks[None, :]
    slots = jax.vmap(lambda k: jax.random.permutation(k, PANEL))(jax.random.split(keys[4], DEVICES)).astype(jnp.int32)
    place = jnp.take_along_axis(entries, slots, axis=1)
    return (pick.reshape(-1), place.reshape(-1))


def draw_a_pick(key, part):
    return layout(key, 11)[0]


def draw_a_place(key, part):
    return layout(key, 11)[1]


def draw_b_pick(key, part):
    return layout(key, 12)[0]


def draw_b_place(key, part):
    return layout(key, 12)[1]


def draw_prod_a(key, part):
    key = jax.random.fold_in(key, 21)
    return jax.random.randint(key, (STEPS, DEVICES * PROD), 0, PANEL, dtype=jnp.int32)


def draw_prod_b(key, part):
    key = jax.random.fold_in(key, 22)
    return jax.random.randint(key, (STEPS, DEVICES * PROD), 0, PANEL, dtype=jnp.int32)


def draw_prod_c(key, part):
    key = jax.random.fold_in(key, 23)
    keys = jax.random.split(key, 4)
    counts = jax.random.randint(keys[0], (STEPS, DEVICES), (PROD + 2) // 3, PROD + 1, dtype=jnp.int32)
    busiest = jax.random.randint(keys[1], (STEPS,), 0, DEVICES, dtype=jnp.int32)
    counts = jnp.where(jnp.arange(DEVICES, dtype=jnp.int32)[None, :] == busiest[:, None], PROD, counts)
    orders = jax.vmap(lambda k: jax.random.permutation(k, PROD))(jax.random.split(keys[2], STEPS * DEVICES)).astype(jnp.int32)
    live = orders < counts.reshape(-1)[:, None]
    targets = jax.random.randint(keys[3], (STEPS * DEVICES, PROD), 0, CBLK, dtype=jnp.int32)
    return jnp.where(live, targets, CBLK).astype(jnp.int32).reshape(STEPS, DEVICES * PROD)


def steps_of(own_key, extent, pieces, smallest, high):
    def one(dim, parts):
        steps = jax.random.uniform(jax.random.fold_in(jax.random.fold_in(own_key, 6), dim), (parts,), jnp.float32, smallest / len(pieces), high / len(pieces))
        return jnp.repeat(jnp.exp(steps), extent[dim] // parts).reshape((-1,) + (1,) * (len(extent) - dim - 1))

    loudness = one(*pieces[0])
    for cut in pieces[1:]:
        loudness = loudness * one(*cut)
    return loudness


def scatter_about(stream_key, extent, spread, bound, cuts=(), kind=jnp.bfloat16):
    loudness = steps_of(stream_key, extent, cuts, -0.22, 0.18) if cuts else 1.0
    drawn = jax.random.normal(stream_key, extent, jnp.float32) * spread * loudness
    return jnp.minimum(jnp.maximum(drawn, -bound), bound).astype(kind)


def setup_inputs(seed: int = 0) -> dict:
    arg_keys = jax.random.split(jax.random.key(seed), 10)
    return {
        "a_blocks": scatter_about(arg_keys[0], (NBLK, BS, BS), (BS * 8) ** -0.5, 0.1875, ((0, 128),), jnp.float32),
        "a_pick": draw_a_pick(jax.random.fold_in(arg_keys[9], 71), 0),
        "a_place": draw_a_place(jax.random.fold_in(arg_keys[9], 71), 0),
        "b_blocks": scatter_about(arg_keys[3], (NBLK, BS, BS), 1.0, 6.0, ((0, 128),), jnp.float32),
        "b_pick": draw_b_pick(jax.random.fold_in(arg_keys[9], 71), 0),
        "b_place": draw_b_place(jax.random.fold_in(arg_keys[9], 71), 0),
        "prod_a": draw_prod_a(jax.random.fold_in(arg_keys[9], 71), 0),
        "prod_b": draw_prod_b(jax.random.fold_in(arg_keys[9], 71), 0),
        "prod_c": draw_prod_c(jax.random.fold_in(arg_keys[9], 71), 0),
    }


def arrange(blocks, pick, place):
    devices = N_ROW * N_COL
    place_rows = place.reshape(devices, PANEL)
    source = place_rows // CAP
    rank = place_rows % CAP
    target = jnp.arange(devices, dtype=jnp.int32)[:, None]
    pick_rows = pick.reshape(devices, devices * CAP)
    local = pick_rows[source, target * CAP + rank]
    index = jnp.where(local < PANEL, source * PANEL + local, NBLK).astype(jnp.int32)
    taken = jnp.take(blocks, index.reshape(-1), axis=0, mode="fill", fill_value=0.0)
    return taken.reshape(devices, PANEL, BS, BS)


def reference(a_blocks, a_pick, a_place, b_blocks, b_pick, b_place, prod_a, prod_b, prod_c):
    devices = N_ROW * N_COL
    panels_a = arrange(a_blocks, a_pick, a_place)
    panels_b = arrange(b_blocks, b_pick, b_place)
    lists_a = prod_a.reshape(STEPS, devices, PROD)
    lists_b = prod_b.reshape(STEPS, devices, PROD)
    lists_c = prod_c.reshape(STEPS, devices, PROD)

    def one_device(device):
        grid_row = device // N_COL
        grid_col = device % N_COL
        total = jnp.zeros((CBLK, BS, BS), jnp.float32)
        for step in range(STEPS):
            owner_a = grid_row * N_COL + (grid_col + step) % N_COL
            owner_b = ((grid_row + step) % N_ROW) * N_COL + grid_col
            left = jnp.take(panels_a[owner_a], lists_a[step, device], axis=0)
            right = jnp.take(panels_b[owner_b], lists_b[step, device], axis=0)
            products = jnp.einsum("pij,pjk->pik", left.astype(jnp.float32), right.astype(jnp.float32), precision=lax.Precision.HIGHEST)
            total = total + jax.ops.segment_sum(products, lists_c[step, device], num_segments=CBLK)
        return total

    result = lax.map(one_device, jnp.arange(devices, dtype=jnp.int32))
    return result.reshape(CTOT, BS, BS)
```

```python
import functools

import jax
import jax.numpy as jnp
from jax import lax
from jax.experimental import pallas as pl
from jax.experimental.pallas import tpu as pltpu
from jax.sharding import PartitionSpec as P

CBLK = 64
CHUNKS = 4
VMEM_LIMIT = 28 * 1024 * 1024

ANY = pl.BlockSpec(memory_space=pl.ANY)
SMEM = pl.BlockSpec(memory_space=pltpu.SMEM)


def permute(array, mapping):
    rows, cols = lax.axis_size("row"), lax.axis_size("col")
    pairs = []
    for r in range(rows):
        for c in range(cols):
            source = mapping(r, c)
            if source is not None:
                pairs.append(((source[0] % rows) * cols + source[1] % cols, r * cols + c))
    return lax.ppermute(array, ("row", "col"), pairs)


def fill_kernel(a_pick, b_pick, a_blocks, b_blocks, out, sem):
    panel = a_blocks.shape[0]
    slots = a_pick.shape[0]

    def body(q, carry):
        pa = a_pick[q]
        pb = b_pick[q]

        @pl.when(pa < panel)
        def _():
            pltpu.make_async_copy(a_blocks.at[pa], out.at[q, 0], sem.at[0]).start()

        @pl.when(pb < panel)
        def _():
            pltpu.make_async_copy(b_blocks.at[pb], out.at[q, 1], sem.at[1]).start()

        return carry

    lax.fori_loop(0, slots, body, 0)
    pltpu.make_async_copy(a_blocks, a_blocks, sem.at[0]).wait()
    pltpu.make_async_copy(b_blocks, b_blocks, sem.at[1]).wait()


def fill(a_pick, b_pick, a_blocks, b_blocks):
    slots = a_pick.shape[0]
    width = a_blocks.shape[1]
    nbytes = 4 * a_blocks.size * 4
    return pl.pallas_call(
        fill_kernel,
        out_shape=jax.ShapeDtypeStruct((slots, 2, width, width), jnp.float32),
        in_specs=[SMEM, SMEM, ANY, ANY],
        out_specs=ANY,
        scratch_shapes=[pltpu.SemaphoreType.DMA((2,))],
        cost_estimate=pl.CostEstimate(flops=0, bytes_accessed=nbytes, transcendentals=0),
        name="fill",
    )(a_pick, b_pick, a_blocks, b_blocks)


def compact_kernel(chunks, a_place, b_place, arrived, *refs):
    a_out = refs[:chunks]
    b_out = refs[chunks]
    sem = refs[chunks + 1]
    part = a_out[0].shape[0]
    for i in range(chunks):

        def body(j, carry, i=i):
            pltpu.make_async_copy(arrived.at[a_place[i * part + j], 0], a_out[i].at[j], sem.at[i]).start()
            return carry

        lax.fori_loop(0, part, body, 0)

    def body_b(j, carry):
        pltpu.make_async_copy(arrived.at[b_place[j], 1], b_out.at[j], sem.at[chunks]).start()
        return carry

    lax.fori_loop(0, b_out.shape[0], body_b, 0)
    for i in range(chunks):
        pltpu.make_async_copy(a_out[i], a_out[i], sem.at[i]).wait()
    pltpu.make_async_copy(b_out, b_out, sem.at[chunks]).wait()


def compact(a_place, b_place, arrived):
    panel = a_place.shape[0]
    width = arrived.shape[-1]
    shapes = [jax.ShapeDtypeStruct((panel // CHUNKS, width, width), jnp.float32)] * CHUNKS
    shapes.append(jax.ShapeDtypeStruct((panel, width, width), jnp.float32))
    outs = pl.pallas_call(
        functools.partial(compact_kernel, CHUNKS),
        out_shape=shapes,
        in_specs=[SMEM, SMEM, ANY],
        out_specs=[ANY] * (CHUNKS + 1),
        scratch_shapes=[pltpu.SemaphoreType.DMA((CHUNKS + 1,))],
        cost_estimate=pl.CostEstimate(flops=0, bytes_accessed=4 * panel * width * width * 4, transcendentals=0),
        name="compact",
    )(a_place, b_place, arrived)
    return list(outs[:CHUNKS]), outs[CHUNKS]


def split(value):
    high = value.astype(jnp.bfloat16)
    low = (value - high.astype(jnp.float32)).astype(jnp.bfloat16)
    return high, low


def block_product(left, right):
    lh, ll = split(left)
    rh, rl = split(right)
    both = jnp.dot(
        jnp.concatenate([lh, ll], axis=1),
        jnp.concatenate([rh, rh], axis=0),
        preferred_element_type=jnp.float32,
    )
    return both + jnp.dot(lh, rl, preferred_element_type=jnp.float32)


def step_kernel(chunks, has_c, n_b, core, index_a, index_b, index_c, *refs):
    a_parts = refs[:chunks]
    b_options = refs[chunks : chunks + n_b]
    refs = refs[chunks + n_b :]
    if has_c:
        c_in, refs = refs[0], refs[1:]
    c_out, a_ref, b_ref, c_ref, sem = refs
    part = a_parts[0].shape[0]
    blocks = c_out.shape[0]

    a_copies = [
        pltpu.make_async_copy(a_parts[i], a_ref.at[pl.ds(i * part, part)], sem.at[i]) for i in range(chunks)
    ]
    for copy in a_copies:
        copy.start()
    if n_b == 1:
        pltpu.make_async_copy(b_options[0], b_ref, sem.at[chunks]).start()
    else:
        for k in range(n_b):

            @pl.when(core[0] == k)
            def _(k=k):
                pltpu.make_async_copy(b_options[k], b_ref, sem.at[chunks]).start()

    if has_c:
        pltpu.make_async_copy(c_in, c_ref.at[pl.ds(0, blocks)], sem.at[chunks + 1]).start()
    else:
        c_ref[...] = jnp.zeros_like(c_ref)
    for copy in a_copies:
        copy.wait()
    pltpu.make_async_copy(b_options[0], b_ref, sem.at[chunks]).wait()
    if has_c:
        pltpu.make_async_copy(c_in, c_ref.at[pl.ds(0, blocks)], sem.at[chunks + 1]).wait()

    def body(e, carry):
        m = index_c[e]

        @pl.when(m < blocks)
        def _():
            c_ref[m] += block_product(a_ref[index_a[e]], b_ref[index_b[e]])

        return carry

    lax.fori_loop(0, index_a.shape[0], body, 0)
    out = pltpu.make_async_copy(c_ref.at[pl.ds(0, blocks)], c_out, sem.at[chunks + 1])
    out.start()
    out.wait()


def step_product(core, index_a, index_b, index_c, a_parts, b_options, total):
    chunks, n_b = len(a_parts), len(b_options)
    part, width, _ = a_parts[0].shape
    panel = b_options[0].shape[0]
    has_c = total is not None
    operands = [core, index_a, index_b, index_c, *a_parts, *b_options]
    in_specs = [SMEM] * 4 + [ANY] * (chunks + n_b)
    aliases = {}
    if has_c:
        aliases = {len(operands): 0}
        operands.append(total)
        in_specs.append(ANY)
    entries = index_a.shape[0]
    return pl.pallas_call(
        functools.partial(step_kernel, chunks, has_c, n_b),
        out_shape=jax.ShapeDtypeStruct((CBLK, width, width), jnp.float32),
        in_specs=in_specs,
        out_specs=ANY,
        scratch_shapes=[
            pltpu.VMEM((panel, width, width), jnp.float32),
            pltpu.VMEM((panel, width, width), jnp.float32),
            pltpu.VMEM((CBLK, width, width), jnp.float32),
            pltpu.SemaphoreType.DMA((chunks + 2,)),
        ],
        input_output_aliases=aliases,
        compiler_params=pltpu.CompilerParams(vmem_limit_bytes=VMEM_LIMIT),
        cost_estimate=pl.CostEstimate(
            flops=6 * entries * width**3, bytes_accessed=4 * 4 * panel * width * width, transcendentals=0
        ),
        name="step",
    )(*operands)


def local(a_blocks, a_pick, a_place, b_blocks, b_pick, b_place, prod_a, prod_b, prod_c):
    core = (lax.axis_index("row") % 2).astype(jnp.int32).reshape(1)
    odd = lax.axis_index("col") % 2 == 1

    outgoing = fill(a_pick, b_pick, a_blocks, b_blocks)
    arrived = lax.all_to_all(outgoing, ("row", "col"), split_axis=0, concat_axis=0, tiled=True)
    a0, b0 = compact(a_place, b_place, arrived)

    a2 = [permute(part, lambda r, c: (r, c + 2)) for part in a0]
    b1 = permute(b0, lambda r, c: (r + 1, c))
    b2_far = permute(b0, lambda r, c: (r + 2, c) if r % 2 else None)
    b3_far = permute(b0, lambda r, c: (r + 3, c) if r % 2 else None)
    a1 = [
        permute(jnp.where(odd, own, far), lambda r, c: (r, c ^ 1)) for own, far in zip(a0, a2)
    ]
    a3 = [permute(part, lambda r, c: (r, c + 2)) for part in a1]
    b2_near = permute(b1, lambda r, c: None if r % 2 else (r + 1, c))
    b3_near = permute(b2_far, lambda r, c: None if r % 2 else (r + 1, c))

    total = step_product(core, prod_a[0], prod_b[0], prod_c[0], a0, [b0], None)
    total = step_product(core, prod_a[2], prod_b[2], prod_c[2], a2, [b2_near, b2_far], total)
    total = step_product(core, prod_a[1], prod_b[1], prod_c[1], a1, [b1], total)
    total = step_product(core, prod_a[3], prod_b[3], prod_c[3], a3, [b3_near, b3_far], total)
    return total


def solution(mesh):
    placed = (
        P(("row", "col"), None, None),
        P(("row", "col")),
        P(("row", "col")),
        P(("row", "col"), None, None),
        P(("row", "col")),
        P(("row", "col")),
        P(None, ("row", "col")),
        P(None, ("row", "col")),
        P(None, ("row", "col")),
    )
    return jax.shard_map(
        local, mesh=mesh, in_specs=placed, out_specs=P(("row", "col"), None, None), check_vma=False
    )
```

```python
import functools

import jax
import jax.numpy as jnp
from jax import lax
from jax.experimental import pallas as pl
from jax.experimental.pallas import tpu as pltpu
from jax.sharding import PartitionSpec as P

CBLK = 64
SIZES = (20, 20, 16)
GROUP = 4
VMEM_LIMIT = 60 * 1024 * 1024

ANY = pl.BlockSpec(memory_space=pl.ANY)
HBM = pl.BlockSpec(memory_space=pltpu.HBM)
SMEM = pl.BlockSpec(memory_space=pltpu.SMEM)


def permute(array, mapping):
    rows, cols = lax.axis_size("row"), lax.axis_size("col")
    pairs = []
    for r in range(rows):
        for c in range(cols):
            source = mapping(r, c)
            if source is not None:
                pairs.append(((source[0] % rows) * cols + source[1] % cols, r * cols + c))
    return lax.ppermute(array, ("row", "col"), pairs)


def fill_kernel(a_pick, b_pick, near_a, near_b, near_c, flags, a_blocks, b_blocks, out, a_ref, b_ref, sem):
    panel = a_blocks.shape[0]
    load_a = pltpu.make_async_copy(a_blocks, a_ref, sem.at[0])
    load_b = pltpu.make_async_copy(b_blocks, b_ref, sem.at[1])
    load_a.start()
    load_b.start()
    for side, (load, pick, held) in enumerate([(load_a, a_pick, a_ref), (load_b, b_pick, b_ref)]):
        load.wait()

        def body(q, carry, side=side, pick=pick, held=held):
            p = pick[q]

            @pl.when(p < panel)
            def _():
                pltpu.make_async_copy(held.at[p], out.at[q, side], sem.at[2 + side]).start()

            return carry

        lax.fori_loop(0, pick.shape[0], body, 0)
    pltpu.make_async_copy(a_blocks, a_ref, sem.at[2]).wait()
    pltpu.make_async_copy(b_blocks, b_ref, sem.at[3]).wait()


def fill(a_pick, b_pick, small, a_blocks, b_blocks):
    slots = a_pick.shape[0]
    panel, width, _ = a_blocks.shape
    return pl.pallas_call(
        fill_kernel,
        out_shape=jax.ShapeDtypeStruct((slots, 2, width, width), jnp.float32),
        in_specs=[SMEM] * 6 + [HBM, HBM],
        out_specs=HBM,
        scratch_shapes=[
            pltpu.VMEM((panel, width, width), jnp.float32),
            pltpu.VMEM((panel, width, width), jnp.float32),
            pltpu.SemaphoreType.DMA((4,)),
        ],
        compiler_params=pltpu.CompilerParams(vmem_limit_bytes=VMEM_LIMIT),
        cost_estimate=pl.CostEstimate(flops=0, bytes_accessed=16 * a_blocks.size, transcendentals=0),
        name="fill",
    )(a_pick, b_pick, *small, a_blocks, b_blocks)


def compact_kernel(a_place, b_place, arrived, a_out, b_out, a_ref, b_ref, in_sem, out_sem):
    sides = [(a_place, a_ref, a_out), (b_place, b_ref, b_out)]
    for side, (place, held, out) in enumerate(sides):

        def body(j, carry, side=side, place=place, held=held):
            pltpu.make_async_copy(arrived.at[place[j], side], held.at[j], in_sem.at[side]).start()
            return carry

        lax.fori_loop(0, place.shape[0], body, 0)
    for side, (place, held, out) in enumerate(sides):
        pltpu.make_async_copy(held, held, in_sem.at[side]).wait()
        pltpu.make_async_copy(held, out, out_sem.at[side]).start()
    for side, (place, held, out) in enumerate(sides):
        pltpu.make_async_copy(held, out, out_sem.at[side]).wait()


def compact(a_place, b_place, arrived):
    panel = a_place.shape[0]
    width = arrived.shape[-1]
    return pl.pallas_call(
        compact_kernel,
        out_shape=[jax.ShapeDtypeStruct((panel, width, width), jnp.float32)] * 2,
        in_specs=[SMEM, SMEM, HBM],
        out_specs=[HBM] * 2,
        scratch_shapes=[
            pltpu.VMEM((panel, width, width), jnp.float32),
            pltpu.VMEM((panel, width, width), jnp.float32),
            pltpu.SemaphoreType.DMA((2,)),
            pltpu.SemaphoreType.DMA((2,)),
        ],
        compiler_params=pltpu.CompilerParams(vmem_limit_bytes=VMEM_LIMIT),
        cost_estimate=pl.CostEstimate(flops=0, bytes_accessed=16 * panel * width * width, transcendentals=0),
        name="compact",
    )(a_place, b_place, arrived)


def split(value):
    high = value.astype(jnp.bfloat16)
    low = (value - high.astype(jnp.float32)).astype(jnp.bfloat16)
    return high, low


def block_product(left, right):
    lh, ll = split(left)
    rh, rl = split(right)
    both = jnp.dot(
        jnp.concatenate([lh, ll], axis=1),
        jnp.concatenate([rh, rh], axis=0),
        preferred_element_type=jnp.float32,
    )
    return both + jnp.dot(lh, rl, preferred_element_type=jnp.float32)


def step_kernel(t, first, parts, options, has_c, flags, index_a, index_b, index_c, *refs):
    a_parts, b_in = refs[:parts], refs[parts : parts + options]
    refs = refs[parts + options :]
    if has_c:
        c_in, refs = refs[0], refs[1:]
    c_out, a_ref, b_ref, c_ref, live, sem = refs
    sizes = [part.shape[0] for part in a_parts]
    last = first + sum(sizes)
    blocks = c_out.shape[0]
    entries = index_a.shape[1]

    copies = [
        pltpu.make_async_copy(a_parts[i], a_ref.at[pl.ds(sum(sizes[:i]), sizes[i])], sem.at[i])
        for i in range(parts)
    ]
    if has_c:
        copies.append(pltpu.make_async_copy(c_in, c_ref, sem.at[parts + 1]))
    for copy in copies:
        copy.start()
    b_copies = [pltpu.make_async_copy(ref, b_ref, sem.at[parts]) for ref in b_in]
    for k, copy in enumerate(b_copies):
        if options == 1:
            copy.start()
        else:
            pl.when(flags[0] == k)(copy.start)

    def listing(e, count):
        live[count] = e
        slot = index_a[t, e]
        used = (index_c[t, e] < blocks) & (slot >= first) & (slot < last)
        return count + jnp.where(used, 1, 0)

    count = lax.fori_loop(0, entries, listing, 0, unroll=4)
    if not has_c:
        c_ref[...] = jnp.zeros_like(c_ref)
    for copy in copies + b_copies[:1]:
        copy.wait()

    def add(at):
        e = live[at]
        c_ref[index_c[t, e]] += block_product(a_ref[index_a[t, e] - first], b_ref[index_b[t, e]])

    def several(g, carry):
        for u in range(GROUP):
            add(g * GROUP + u)
        return carry

    def single(at, carry):
        add(at)
        return carry

    groups = count // GROUP
    lax.fori_loop(0, groups, several, 0)
    lax.fori_loop(groups * GROUP, count, single, 0)
    out = pltpu.make_async_copy(c_ref, c_out, sem.at[parts + 1])
    out.start()
    out.wait()


def step_product(t, flags, prods, first, a_parts, b_in, total):
    parts, options = len(a_parts), len(b_in)
    held = sum(part.shape[0] for part in a_parts)
    width = a_parts[0].shape[1]
    panel = b_in[0].shape[0]
    has_c = total is not None
    operands = [flags, *prods, *a_parts, *b_in]
    in_specs = [SMEM] * 4 + [ANY] * (parts + options)
    aliases = {}
    if has_c:
        aliases = {len(operands): 0}
        operands.append(total)
        in_specs.append(ANY)
    entries = prods[0].shape[1]
    return pl.pallas_call(
        functools.partial(step_kernel, t, first, parts, options, has_c),
        out_shape=jax.ShapeDtypeStruct((CBLK, width, width), jnp.float32),
        in_specs=in_specs,
        out_specs=ANY,
        scratch_shapes=[
            pltpu.VMEM((held, width, width), jnp.float32),
            pltpu.VMEM((panel, width, width), jnp.float32),
            pltpu.VMEM((CBLK, width, width), jnp.float32),
            pltpu.SMEM((entries + 1,), jnp.int32),
            pltpu.SemaphoreType.DMA((parts + 2,)),
        ],
        input_output_aliases=aliases,
        compiler_params=pltpu.CompilerParams(vmem_limit_bytes=VMEM_LIMIT),
        cost_estimate=pl.CostEstimate(
            flops=6000 * entries * width**3, bytes_accessed=16 * panel * width * width, transcendentals=0
        ),
        name="step",
    )(*operands)


def together(*values):
    return lax.optimization_barrier(values)


def local(a_blocks, a_pick, a_place, b_blocks, b_pick, b_place, prod_a, prod_b, prod_c):
    flags = jnp.stack([lax.axis_index("row") % 2, lax.axis_index("col") % 2]).astype(jnp.int32)
    prods = (prod_a, prod_b, prod_c)
    outgoing = fill(a_pick, b_pick, (*prods, flags), a_blocks, b_blocks)
    arrived = lax.all_to_all(outgoing, ("row", "col"), split_axis=0, concat_axis=0, tiled=True)
    a0, b0 = compact(a_place, b_place, arrived)
    a0, b0, flags = together(a0, b0, flags)
    upper, odd = flags[0] == 1, flags[1] == 1

    step = functools.partial(step_product, flags=flags, prods=prods)
    a2 = permute(a0, lambda r, c: (r, c + 2))
    b1 = permute(b0, lambda r, c: (r + 1, c))
    b3_even = permute(b0, lambda r, c: None if r % 2 else (r + 3, c))
    total = step(0, first=0, a_parts=[a0], b_in=[b0], total=None)
    a0, a2, b0, b1, b3_even, total = together(a0, a2, b0, b1, b3_even, total)

    firsts = [sum(SIZES[:i]) for i in range(len(SIZES))]
    a1 = []
    for first, size in zip(firsts, SIZES):
        rows = slice(first, first + size)
        a1.append(permute(jnp.where(odd, a0[rows], a2[rows]), lambda r, c: (r, c ^ 1)))
    b2 = permute(jnp.where(upper, b1, b3_even), lambda r, c: (r ^ 1, c))
    b3_odd = permute(b0, lambda r, c: (r + 3, c) if r % 2 else None)
    total = step(2, first=0, a_parts=[a2], b_in=[b2], total=total)
    a1[-1], total = together(a1[-1], total)
    a3 = [permute(part, lambda r, c: (r, c + 2)) for part in a1]
    total = step(1, first=0, a_parts=a1, b_in=[b1], total=total)
    for first, part in zip(firsts, a3):
        total = step(3, first=first, a_parts=[part], b_in=[b3_even, b3_odd], total=total)
    return total


def solution(mesh):
    placed = (
        P(("row", "col"), None, None),
        P(("row", "col")),
        P(("row", "col")),
        P(("row", "col"), None, None),
        P(("row", "col")),
        P(("row", "col")),
        P(None, ("row", "col")),
        P(None, ("row", "col")),
        P(None, ("row", "col")),
    )
    return jax.shard_map(
        local, mesh=mesh, in_specs=placed, out_specs=P(("row", "col"), None, None), check_vma=False
    )
```

```python
import functools

import jax
import jax.numpy as jnp
from jax import lax
from jax.experimental import pallas as pl
from jax.experimental.pallas import tpu as pltpu
from jax.sharding import PartitionSpec as P

CBLK = 64
SIZES = (14, 14, 14, 14)
GROUP = 4
VMEM_LIMIT = 60 * 1024 * 1024

ANY = pl.BlockSpec(memory_space=pl.ANY)
HBM = pl.BlockSpec(memory_space=pltpu.HBM)
SMEM = pl.BlockSpec(memory_space=pltpu.SMEM)


def permute(array, mapping):
    rows, cols = lax.axis_size("row"), lax.axis_size("col")
    pairs = []
    for r in range(rows):
        for c in range(cols):
            source = mapping(r, c)
            if source is not None:
                pairs.append(((source[0] % rows) * cols + source[1] % cols, r * cols + c))
    return lax.ppermute(array, ("row", "col"), pairs)


def fill_kernel(a_pick, b_pick, near_a, near_b, near_c, flags, a_blocks, b_blocks, out, a_ref, b_ref, sem):
    panel = a_blocks.shape[0]
    load_a = pltpu.make_async_copy(a_blocks, a_ref, sem.at[0])
    load_b = pltpu.make_async_copy(b_blocks, b_ref, sem.at[1])
    load_a.start()
    load_b.start()
    for side, (load, pick, held) in enumerate([(load_a, a_pick, a_ref), (load_b, b_pick, b_ref)]):
        load.wait()

        def body(q, carry, side=side, pick=pick, held=held):
            p = pick[q]

            @pl.when(p < panel)
            def _():
                pltpu.make_async_copy(held.at[p], out.at[q, side], sem.at[2 + side]).start()

            return carry

        lax.fori_loop(0, pick.shape[0], body, 0)
    pltpu.make_async_copy(a_blocks, a_ref, sem.at[2]).wait()
    pltpu.make_async_copy(b_blocks, b_ref, sem.at[3]).wait()


def fill(a_pick, b_pick, small, a_blocks, b_blocks):
    slots = a_pick.shape[0]
    panel, width, _ = a_blocks.shape
    return pl.pallas_call(
        fill_kernel,
        out_shape=jax.ShapeDtypeStruct((slots, 2, width, width), jnp.float32),
        in_specs=[SMEM] * 6 + [HBM, HBM],
        out_specs=HBM,
        scratch_shapes=[
            pltpu.VMEM((panel, width, width), jnp.float32),
            pltpu.VMEM((panel, width, width), jnp.float32),
            pltpu.SemaphoreType.DMA((4,)),
        ],
        compiler_params=pltpu.CompilerParams(vmem_limit_bytes=VMEM_LIMIT),
        cost_estimate=pl.CostEstimate(flops=0, bytes_accessed=16 * a_blocks.size, transcendentals=0),
        name="fill",
    )(a_pick, b_pick, *small, a_blocks, b_blocks)


def compact_kernel(a_place, b_place, arrived, a_out, b_out, a_ref, b_ref, in_sem, out_sem):
    sides = [(a_place, a_ref, a_out), (b_place, b_ref, b_out)]
    for side, (place, held, out) in enumerate(sides):

        def body(j, carry, side=side, place=place, held=held):
            pltpu.make_async_copy(arrived.at[place[j], side], held.at[j], in_sem.at[side]).start()
            return carry

        lax.fori_loop(0, place.shape[0], body, 0)
    for side, (place, held, out) in enumerate(sides):
        pltpu.make_async_copy(held, held, in_sem.at[side]).wait()
        pltpu.make_async_copy(held, out, out_sem.at[side]).start()
    for side, (place, held, out) in enumerate(sides):
        pltpu.make_async_copy(held, out, out_sem.at[side]).wait()


def compact(a_place, b_place, arrived):
    panel = a_place.shape[0]
    width = arrived.shape[-1]
    return pl.pallas_call(
        compact_kernel,
        out_shape=[jax.ShapeDtypeStruct((panel, width, width), jnp.float32)] * 2,
        in_specs=[SMEM, SMEM, HBM],
        out_specs=[HBM] * 2,
        scratch_shapes=[
            pltpu.VMEM((panel, width, width), jnp.float32),
            pltpu.VMEM((panel, width, width), jnp.float32),
            pltpu.SemaphoreType.DMA((2,)),
            pltpu.SemaphoreType.DMA((2,)),
        ],
        compiler_params=pltpu.CompilerParams(vmem_limit_bytes=VMEM_LIMIT),
        cost_estimate=pl.CostEstimate(flops=0, bytes_accessed=16 * panel * width * width, transcendentals=0),
        name="compact",
    )(a_place, b_place, arrived)


def split(value):
    high = value.astype(jnp.bfloat16)
    low = (value - high.astype(jnp.float32)).astype(jnp.bfloat16)
    return high, low


def block_product(left, right):
    lh, ll = split(left)
    rh, rl = split(right)
    both = jnp.dot(
        jnp.concatenate([lh, ll], axis=1),
        jnp.concatenate([rh, rh], axis=0),
        preferred_element_type=jnp.float32,
    )
    return both + jnp.dot(lh, rl, preferred_element_type=jnp.float32)


def products_kernel(jobs, has_c, flags, index_a, index_b, index_c, *refs):
    refs = list(refs)
    sources = []
    for _, _, sizes, options in jobs:
        sources.append((refs[: len(sizes)], refs[len(sizes) : len(sizes) + options]))
        del refs[: len(sizes) + options]
    c_in = refs.pop(0) if has_c else None
    c_out = refs.pop(0)
    held = [(refs[2 * n], refs[2 * n + 1]) for n in range(len(jobs))]
    c_ref, live, sem = refs[2 * len(jobs) :]
    blocks = c_out.shape[0]
    entries = index_a.shape[1]

    if has_c:
        load_c = pltpu.make_async_copy(c_in, c_ref, sem.at[len(jobs), 0])
        load_c.start()
    waits = []
    for n, (_, _, sizes, options) in enumerate(jobs):
        a_ref, b_ref = held[n]
        a_parts, b_in = sources[n]
        copies = [
            pltpu.make_async_copy(part, a_ref.at[pl.ds(sum(sizes[:i]), sizes[i])], sem.at[n, i])
            for i, part in enumerate(a_parts)
        ]
        for copy in copies:
            copy.start()
        b_copies = [pltpu.make_async_copy(ref, b_ref, sem.at[n, len(sizes)]) for ref in b_in]
        for k, copy in enumerate(b_copies):
            if options == 1:
                copy.start()
            else:
                pl.when(flags[0] == k)(copy.start)
        waits.append(copies + b_copies[:1])

    counts = []
    for n, (t, first, sizes, _) in enumerate(jobs):

        def listing(e, count, n=n, t=t, first=first, last=first + sum(sizes)):
            live[n, count] = e
            slot = index_a[t, e]
            used = (index_c[t, e] < blocks) & (slot >= first) & (slot < last)
            return count + jnp.where(used, 1, 0)

        counts.append(lax.fori_loop(0, entries, listing, 0, unroll=4))
    if has_c:
        load_c.wait()
    else:
        c_ref[...] = jnp.zeros_like(c_ref)

    for n, (t, first, _, _) in enumerate(jobs):
        a_ref, b_ref = held[n]
        for copy in waits[n]:
            copy.wait()

        def add(at, n=n, t=t, first=first, a_ref=a_ref, b_ref=b_ref):
            e = live[n, at]
            c_ref[index_c[t, e]] += block_product(a_ref[index_a[t, e] - first], b_ref[index_b[t, e]])

        def several(g, carry, add=add):
            for u in range(GROUP):
                add(g * GROUP + u)
            return carry

        def single(at, carry, add=add):
            add(at)
            return carry

        groups = counts[n] // GROUP
        lax.fori_loop(0, groups, several, 0)
        lax.fori_loop(groups * GROUP, counts[n], single, 0)
    out = pltpu.make_async_copy(c_ref, c_out, sem.at[len(jobs), 0])
    out.start()
    out.wait()


def products(flags, prods, jobs, total):
    entries = prods[0].shape[1]
    width = jobs[0][2][0].shape[1]
    has_c = total is not None
    operands = [flags, *prods]
    scratch = []
    static = []
    for t, first, parts, b_in in jobs:
        operands += [*parts, *b_in]
        sizes = tuple(part.shape[0] for part in parts)
        static.append((t, first, sizes, len(b_in)))
        scratch.append(pltpu.VMEM((sum(sizes), width, width), jnp.float32))
        scratch.append(pltpu.VMEM(b_in[0].shape, jnp.float32))
    aliases = {}
    if has_c:
        aliases = {len(operands): 0}
        operands.append(total)
    slots = max(len(sizes) for _, _, sizes, _ in static) + 1
    return pl.pallas_call(
        functools.partial(products_kernel, tuple(static), has_c),
        out_shape=jax.ShapeDtypeStruct((CBLK, width, width), jnp.float32),
        in_specs=[SMEM] * 4 + [ANY] * (len(operands) - 4),
        out_specs=ANY,
        scratch_shapes=scratch
        + [
            pltpu.VMEM((CBLK, width, width), jnp.float32),
            pltpu.SMEM((len(jobs), entries + 1), jnp.int32),
            pltpu.SemaphoreType.DMA((len(jobs) + 1, slots)),
        ],
        input_output_aliases=aliases,
        compiler_params=pltpu.CompilerParams(vmem_limit_bytes=VMEM_LIMIT),
        cost_estimate=pl.CostEstimate(
            flops=6000 * entries * width**3, bytes_accessed=8 * CBLK * width * width, transcendentals=0
        ),
        name="products",
    )(*operands)


def last_kernel(t, first, options, flags, index_a, index_b, index_c, *refs):
    a_in, b_in = refs[0], refs[1 : 1 + options]
    c_in, c_out, a_ref, b_ref, c_ref, live, place, sem = refs[1 + options :]
    blocks = c_out.shape[0]
    entries = index_a.shape[1]
    size = a_in.shape[0]

    def clear(m, carry):
        place[m] = -1
        return carry

    lax.fori_loop(0, blocks, clear, 0, unroll=8)

    def fetch(e, counts):
        slot, m = index_a[t, e] - first, index_c[t, e]
        used = (m < blocks) & (slot >= 0) & (slot < size)
        count, kept = counts
        new = used & (place[jnp.minimum(m, blocks - 1)] < 0)

        @pl.when(used)
        def _():
            live[count] = e
            pltpu.make_async_copy(a_in.at[slot], a_ref.at[count], sem.at[0]).start()
            for k, ref in enumerate(b_in):

                @pl.when(flags[0] == k)
                def _(ref=ref):
                    pltpu.make_async_copy(ref.at[index_b[t, e]], b_ref.at[count], sem.at[0]).start()

        @pl.when(new)
        def _():
            place[m] = kept
            live[entries + kept] = m
            pltpu.make_async_copy(c_in.at[m], c_ref.at[kept], sem.at[0]).start()

        return count + jnp.where(used, 1, 0), kept + jnp.where(new, 1, 0)

    count, kept = lax.fori_loop(0, entries, fetch, (0, 0))

    def arrive(_, carry):
        pltpu.make_async_copy(c_in.at[0], c_ref.at[0], sem.at[0]).wait()
        return carry

    lax.fori_loop(0, 2 * count + kept, arrive, 0)

    def add(at):
        c_ref[place[index_c[t, live[at]]]] += block_product(a_ref[at], b_ref[at])

    def several(g, carry):
        for u in range(GROUP):
            add(g * GROUP + u)
        return carry

    def single(at, carry):
        add(at)
        return carry

    groups = count // GROUP
    lax.fori_loop(0, groups, several, 0)
    lax.fori_loop(groups * GROUP, count, single, 0)

    def store(k, carry):
        pltpu.make_async_copy(c_ref.at[k], c_out.at[live[entries + k]], sem.at[1]).start()
        return carry

    lax.fori_loop(0, kept, store, 0)

    def leave(_, carry):
        pltpu.make_async_copy(c_ref.at[0], c_out.at[0], sem.at[1]).wait()
        return carry

    lax.fori_loop(0, kept, leave, 0)


def last_products(flags, prods, t, first, a_in, b_in, total):
    entries = prods[0].shape[1]
    block = a_in.shape[1:]
    operands = [flags, *prods, a_in, *b_in, total]
    return pl.pallas_call(
        functools.partial(last_kernel, t, first, len(b_in)),
        out_shape=jax.ShapeDtypeStruct(total.shape, jnp.float32),
        in_specs=[SMEM] * 4 + [ANY] * (len(operands) - 4),
        out_specs=ANY,
        scratch_shapes=[
            pltpu.VMEM((entries, *block), jnp.float32),
            pltpu.VMEM((entries, *block), jnp.float32),
            pltpu.VMEM((total.shape[0], *block), jnp.float32),
            pltpu.SMEM((entries + total.shape[0],), jnp.int32),
            pltpu.SMEM((total.shape[0],), jnp.int32),
            pltpu.SemaphoreType.DMA((2,)),
        ],
        input_output_aliases={len(operands) - 1: 0},
        compiler_params=pltpu.CompilerParams(vmem_limit_bytes=VMEM_LIMIT),
        cost_estimate=pl.CostEstimate(
            flops=6000 * entries * block[0] ** 3, bytes_accessed=8 * total.size, transcendentals=0
        ),
        name="last_products",
    )(*operands)


def together(*values):
    return lax.optimization_barrier(values)


def local(a_blocks, a_pick, a_place, b_blocks, b_pick, b_place, prod_a, prod_b, prod_c):
    flags = jnp.stack([lax.axis_index("row") % 2, lax.axis_index("col") % 2]).astype(jnp.int32)
    prods = (prod_a, prod_b, prod_c)
    outgoing = fill(a_pick, b_pick, (*prods, flags), a_blocks, b_blocks)
    arrived = lax.all_to_all(outgoing, ("row", "col"), split_axis=0, concat_axis=0, tiled=True)
    a0, b0 = compact(a_place, b_place, arrived)
    a0, b0, flags = together(a0, b0, flags)
    upper, odd = flags[0] == 1, flags[1] == 1

    add = functools.partial(products, flags, prods)
    a2 = permute(a0, lambda r, c: (r, c + 2))
    b1 = permute(b0, lambda r, c: (r + 1, c))
    b3_even = permute(b0, lambda r, c: None if r % 2 else (r + 3, c))
    total = add([(0, 0, [a0], [b0])], None)
    a0, a2, b0, b1, b3_even, total = together(a0, a2, b0, b1, b3_even, total)

    firsts = [sum(SIZES[:i]) for i in range(len(SIZES))]
    cross = []
    for first, size in zip(firsts, SIZES):
        rows = slice(first, first + size)
        cross.append(jnp.where(odd, a0[rows], a2[rows]))
        if first == 0:
            a0, a2, cross[0] = together(a0, a2, cross[0])
    b1, b3_even, cross[0] = together(b1, b3_even, cross[0])
    a1 = [permute(part, lambda r, c: (r, c ^ 1)) for part in cross]
    b2 = permute(jnp.where(upper, b1, b3_even), lambda r, c: (r ^ 1, c))
    b0, a1[0] = together(b0, a1[0])
    b3_odd = permute(b0, lambda r, c: (r + 3, c) if r % 2 else None)
    b3 = [b3_even, b3_odd]
    a3 = []

    def onward():
        a3.append(permute(a1[len(a3)], lambda r, c: (r, c + 2)))

    onward()
    total = add([(2, 0, [a2], [b2])], total)
    a1[1], total = together(a1[1], total)
    onward()
    total = add([(1, 0, a1[:2], [b1])], total)
    a1[2], total = together(a1[2], total)
    onward()
    total = add([(3, 0, a3[:1], b3)], total)
    a1[3], total = together(a1[3], total)
    onward()
    total = add([(1, firsts[2], a1[2:], [b1]), (3, firsts[1], a3[1:3], b3)], total)
    return last_products(flags, prods, 3, firsts[3], a3[3], b3, total)


def solution(mesh):
    placed = (
        P(("row", "col"), None, None),
        P(("row", "col")),
        P(("row", "col")),
        P(("row", "col"), None, None),
        P(("row", "col")),
        P(("row", "col")),
        P(None, ("row", "col")),
        P(None, ("row", "col")),
        P(None, ("row", "col")),
    )
    return jax.shard_map(
        local, mesh=mesh, in_specs=placed, out_specs=P(("row", "col"), None, None), check_vma=False
    )
```

```python
import functools

import jax
import jax.numpy as jnp
from jax import lax
from jax.experimental import pallas as pl
from jax.experimental.pallas import tpu as pltpu
from jax.sharding import PartitionSpec as P

CBLK = 64
AHEAD = 3
SIZES = (20, 20, 16)
GROUP = 4
VMEM_LIMIT = 60 * 1024 * 1024

ANY = pl.BlockSpec(memory_space=pl.ANY)
HBM = pl.BlockSpec(memory_space=pltpu.HBM)
SMEM = pl.BlockSpec(memory_space=pltpu.SMEM)


def permute(array, mapping):
    rows, cols = lax.axis_size("row"), lax.axis_size("col")
    pairs = []
    for r in range(rows):
        for c in range(cols):
            source = mapping(r, c)
            if source is not None:
                pairs.append(((source[0] % rows) * cols + source[1] % cols, r * cols + c))
    return lax.ppermute(array, ("row", "col"), pairs)


def fill_kernel(cols, a_pick, b_pick, near_a, near_b, near_c, flags, a_blocks, b_blocks, out, a_ref, b_ref, sem):
    panel = a_blocks.shape[0]
    half = a_blocks.shape[1] // 2
    load_a = pltpu.make_async_copy(a_blocks, a_ref, sem.at[0])
    load_b = pltpu.make_async_copy(b_blocks, b_ref, sem.at[1])
    load_a.start()
    load_b.start()
    upper, lower = pl.ds(0, half), pl.ds(half, half)

    def fill_a(q, carry):
        p = a_pick[q]
        col = lax.rem(q, cols)
        behind = q - col + lax.rem(col + cols - AHEAD, cols)

        @pl.when(p < panel)
        def _():
            pltpu.make_async_copy(a_ref.at[p, upper], out.at[q, 0, upper], sem.at[2]).start()
            pltpu.make_async_copy(a_ref.at[p, lower], out.at[behind, 0, lower], sem.at[2]).start()

        return carry

    def fill_b(q, carry):
        p = b_pick[q]

        @pl.when(p < panel)
        def _():
            pltpu.make_async_copy(b_ref.at[p], out.at[q, 1], sem.at[3]).start()

        return carry

    load_a.wait()
    lax.fori_loop(0, a_pick.shape[0], fill_a, 0)
    load_b.wait()
    lax.fori_loop(0, b_pick.shape[0], fill_b, 0)
    pltpu.make_async_copy(a_blocks, a_ref, sem.at[2]).wait()
    pltpu.make_async_copy(b_blocks, b_ref, sem.at[3]).wait()


def fill(cols, a_pick, b_pick, small, a_blocks, b_blocks):
    slots = a_pick.shape[0]
    panel, width, _ = a_blocks.shape
    return pl.pallas_call(
        functools.partial(fill_kernel, cols),
        out_shape=jax.ShapeDtypeStruct((slots, 2, width, width), jnp.float32),
        in_specs=[SMEM] * 6 + [HBM, HBM],
        out_specs=HBM,
        scratch_shapes=[
            pltpu.VMEM((panel, width, width), jnp.float32),
            pltpu.VMEM((panel, width, width), jnp.float32),
            pltpu.SemaphoreType.DMA((4,)),
        ],
        compiler_params=pltpu.CompilerParams(vmem_limit_bytes=VMEM_LIMIT),
        cost_estimate=pl.CostEstimate(flops=0, bytes_accessed=16 * a_blocks.size, transcendentals=0),
        name="fill",
    )(a_pick, b_pick, *small, a_blocks, b_blocks)


def compact_kernel(a_place, far_place, b_place, arrived, up_out, low_out, b_out, up_ref, low_ref, b_ref, in_sem, out_sem):
    half = up_out.shape[1]
    sides = [
        (a_place, 0, pl.ds(0, half), up_ref, up_out),
        (far_place, 0, pl.ds(half, half), low_ref, low_out),
        (b_place, 1, pl.ds(0, 2 * half), b_ref, b_out),
    ]
    for n, (place, side, rows, held, out) in enumerate(sides):

        def body(j, carry, n=n, place=place, side=side, rows=rows, held=held):
            pltpu.make_async_copy(arrived.at[place[j], side, rows], held.at[j], in_sem.at[n]).start()
            return carry

        lax.fori_loop(0, place.shape[0], body, 0, unroll=4)
    for n, (place, side, rows, held, out) in enumerate(sides):
        pltpu.make_async_copy(held, held, in_sem.at[n]).wait()
        pltpu.make_async_copy(held, out, out_sem.at[n]).start()
    for n, (place, side, rows, held, out) in enumerate(sides):
        pltpu.make_async_copy(held, out, out_sem.at[n]).wait()


def compact(a_place, far_place, b_place, arrived):
    panel = a_place.shape[0]
    width = arrived.shape[-1]
    shapes = [(panel, width // 2, width), (panel, width // 2, width), (panel, width, width)]
    return pl.pallas_call(
        compact_kernel,
        out_shape=[jax.ShapeDtypeStruct(shape, jnp.float32) for shape in shapes],
        in_specs=[SMEM, SMEM, SMEM, HBM],
        out_specs=[HBM] * 3,
        scratch_shapes=[pltpu.VMEM(shape, jnp.float32) for shape in shapes]
        + [pltpu.SemaphoreType.DMA((3,)), pltpu.SemaphoreType.DMA((3,))],
        compiler_params=pltpu.CompilerParams(vmem_limit_bytes=VMEM_LIMIT),
        cost_estimate=pl.CostEstimate(flops=0, bytes_accessed=16 * panel * width * width, transcendentals=0),
        name="compact",
    )(a_place, far_place, b_place, arrived)


def split(value):
    high = value.astype(jnp.bfloat16)
    low = (value - high.astype(jnp.float32)).astype(jnp.bfloat16)
    return high, low


def block_product(left, right):
    lh, ll = split(left)
    rh, rl = split(right)
    both = jnp.dot(
        jnp.concatenate([lh, ll], axis=1),
        jnp.concatenate([rh, rh], axis=0),
        preferred_element_type=jnp.float32,
    )
    return both + jnp.dot(lh, rl, preferred_element_type=jnp.float32)


def rows_of(ref, spec):
    if spec is None:
        return ref
    if len(spec) == 3:
        return ref.at[spec[0], pl.ds(spec[1], spec[2])]
    return ref.at[pl.ds(spec[0], spec[1])]


def products_kernel(jobs, has_c, flags, index_a, index_b, index_c, *refs):
    refs, scratch = refs[: len(refs) - len(jobs) * 2 - 3], refs[len(refs) - len(jobs) * 2 - 3 :]
    held = [(scratch[2 * n], scratch[2 * n + 1]) for n in range(len(jobs))]
    c_ref, live, sem = scratch[2 * len(jobs) :]
    c_out = refs[-1]
    blocks = c_out.shape[0]
    entries = index_a.shape[1]
    half = c_ref.shape[1] // 2

    if has_c:
        load_c = pltpu.make_async_copy(refs[-2], c_ref, sem.at[len(jobs), 0])
        load_c.start()
    waits = []
    for n, (_, _, _, upper, lower, b) in enumerate(jobs):
        a_ref, b_ref = held[n]
        copies = [
            pltpu.make_async_copy(rows_of(refs[upper[0]], upper[1]), a_ref.at[:, pl.ds(0, half)], sem.at[n, 0]),
            pltpu.make_async_copy(rows_of(refs[lower[0]], lower[1]), a_ref.at[:, pl.ds(half, half)], sem.at[n, 1]),
        ]
        for copy in copies:
            copy.start()
        for k, source in enumerate(b):
            copy = pltpu.make_async_copy(refs[source], b_ref, sem.at[n, 2])
            if len(b) == 1:
                copy.start()
            else:
                pl.when(flags[0] == k)(copy.start)
        waits.append([*copies, copy])

    counts = []
    for n, (t, first, size, _, _, _) in enumerate(jobs):

        def listing(e, count, n=n, t=t, first=first, size=size):
            live[n, count] = e
            slot = index_a[t, e]
            used = (index_c[t, e] < blocks) & (slot >= first) & (slot < first + size)
            return count + jnp.where(used, 1, 0)

        counts.append(lax.fori_loop(0, entries, listing, 0, unroll=4))
    if has_c:
        load_c.wait()
    else:
        c_ref[...] = jnp.zeros_like(c_ref)

    for n, (t, first, _, _, _, _) in enumerate(jobs):
        a_ref, b_ref = held[n]
        for copy in waits[n]:
            copy.wait()

        def add(at, n=n, t=t, first=first, a_ref=a_ref, b_ref=b_ref):
            e = live[n, at]
            c_ref[index_c[t, e]] += block_product(a_ref[index_a[t, e] - first], b_ref[index_b[t, e]])

        def several(g, carry, add=add):
            for u in range(GROUP):
                add(g * GROUP + u)
            return carry

        def single(at, carry, add=add):
            add(at)
            return carry

        groups = counts[n] // GROUP
        lax.fori_loop(0, groups, several, 0)
        lax.fori_loop(groups * GROUP, counts[n], single, 0)
    out = pltpu.make_async_copy(c_ref, c_out, sem.at[len(jobs), 0])
    out.start()
    out.wait()


def products(flags, prods, jobs, total):
    entries = prods[0].shape[1]
    width = jobs[0][5][0].shape[1]
    has_c = total is not None
    arrays = []

    def number(array):
        for n, known in enumerate(arrays):
            if known is array:
                return n
        arrays.append(array)
        return len(arrays) - 1

    static = []
    scratch = []
    for t, first, size, upper, lower, b in jobs:
        static.append((t, first, size, (number(upper[0]), upper[1]), (number(lower[0]), lower[1]), tuple(number(x) for x in b)))
        scratch.append(pltpu.VMEM((size, width, width), jnp.float32))
        scratch.append(pltpu.VMEM(b[0].shape, jnp.float32))
    operands = [flags, *prods, *arrays]
    aliases = {}
    if has_c:
        aliases = {len(operands): 0}
        operands.append(total)
    return pl.pallas_call(
        functools.partial(products_kernel, tuple(static), has_c),
        out_shape=jax.ShapeDtypeStruct((CBLK, width, width), jnp.float32),
        in_specs=[SMEM] * 4 + [ANY] * (len(operands) - 4),
        out_specs=ANY,
        scratch_shapes=scratch
        + [
            pltpu.VMEM((CBLK, width, width), jnp.float32),
            pltpu.SMEM((len(jobs), entries + 1), jnp.int32),
            pltpu.SemaphoreType.DMA((len(jobs) + 1, 3)),
        ],
        input_output_aliases=aliases,
        compiler_params=pltpu.CompilerParams(vmem_limit_bytes=VMEM_LIMIT),
        cost_estimate=pl.CostEstimate(
            flops=6000 * entries * width**3, bytes_accessed=8 * CBLK * width * width, transcendentals=0
        ),
        name="products",
    )(*operands)


def last_kernel(jobs, flags, index_a, index_b, index_c, *refs):
    c_in, c_out, a_ref, b_ref, c_ref, live, place, sem = refs[len(refs) - 8 :]
    blocks = c_out.shape[0]
    entries = index_a.shape[1]
    half = c_ref.shape[1] // 2
    room = len(jobs) * entries

    def clear(m, carry):
        place[m] = -1
        return carry

    lax.fori_loop(0, blocks, clear, 0, unroll=8)

    counts = (0, 0)
    for t, first, size, upper, lower, b in jobs:

        def fetch(e, counts, t=t, first=first, size=size, upper=upper, lower=lower, b=b):
            slot, m = index_a[t, e] - first, index_c[t, e]
            used = (m < blocks) & (slot >= 0) & (slot < size)
            count, kept = counts
            new = used & (place[jnp.minimum(m, blocks - 1)] < 0)

            @pl.when(used)
            def _():
                live[count] = m
                for part, (n, spec) in enumerate((upper, lower)):
                    source = rows_of(refs[n], spec).at[slot]
                    target = a_ref.at[count, pl.ds(part * half, half)]
                    pltpu.make_async_copy(source, target, sem.at[0]).start()
                for k, n in enumerate(b):
                    copy = pltpu.make_async_copy(refs[n].at[index_b[t, e]], b_ref.at[count], sem.at[0])
                    if len(b) == 1:
                        copy.start()
                    else:
                        pl.when(flags[0] == k)(copy.start)

            @pl.when(new)
            def _():
                place[m] = kept
                live[room + kept] = m
                pltpu.make_async_copy(c_in.at[m], c_ref.at[kept], sem.at[0]).start()

            return count + jnp.where(used, 1, 0), kept + jnp.where(new, 1, 0)

        counts = lax.fori_loop(0, entries, fetch, counts)
    count, kept = counts

    def arrive(_, carry):
        pltpu.make_async_copy(c_in.at[0], c_ref.at[0], sem.at[0]).wait()
        return carry

    lax.fori_loop(0, 2 * count + kept, arrive, 0)

    def add(at):
        c_ref[place[live[at]]] += block_product(a_ref[at], b_ref[at])

    def several(g, carry):
        for u in range(GROUP):
            add(g * GROUP + u)
        return carry

    def single(at, carry):
        add(at)
        return carry

    groups = count // GROUP
    lax.fori_loop(0, groups, several, 0)
    lax.fori_loop(groups * GROUP, count, single, 0)

    def store(k, carry):
        pltpu.make_async_copy(c_ref.at[k], c_out.at[live[room + k]], sem.at[1]).start()
        return carry

    lax.fori_loop(0, kept, store, 0)

    def leave(_, carry):
        pltpu.make_async_copy(c_ref.at[0], c_out.at[0], sem.at[1]).wait()
        return carry

    lax.fori_loop(0, kept, leave, 0)


def last_products(flags, prods, jobs, total):
    entries = prods[0].shape[1]
    block = total.shape[1:]
    arrays = []
    static = []
    for t, first, size, upper, lower, b in jobs:
        n = len(arrays)
        arrays += [upper[0], lower[0], *b]
        static.append((t, first, size, (n, upper[1]), (n + 1, lower[1]), tuple(range(n + 2, len(arrays)))))
    operands = [flags, *prods, *arrays, total]
    room = len(jobs) * entries
    return pl.pallas_call(
        functools.partial(last_kernel, tuple(static)),
        out_shape=jax.ShapeDtypeStruct(total.shape, jnp.float32),
        in_specs=[SMEM] * 4 + [ANY] * (len(operands) - 4),
        out_specs=ANY,
        scratch_shapes=[
            pltpu.VMEM((room, *block), jnp.float32),
            pltpu.VMEM((room, *block), jnp.float32),
            pltpu.VMEM((total.shape[0], *block), jnp.float32),
            pltpu.SMEM((room + total.shape[0],), jnp.int32),
            pltpu.SMEM((total.shape[0],), jnp.int32),
            pltpu.SemaphoreType.DMA((2,)),
        ],
        input_output_aliases={len(operands) - 1: 0},
        compiler_params=pltpu.CompilerParams(vmem_limit_bytes=VMEM_LIMIT),
        cost_estimate=pl.CostEstimate(
            flops=6000 * entries * block[0] ** 3, bytes_accessed=8 * total.size, transcendentals=0
        ),
        name="last_products",
    )(*operands)


def together(*values):
    return lax.optimization_barrier(values)


def local(a_blocks, a_pick, a_place, b_blocks, b_pick, b_place, prod_a, prod_b, prod_c):
    flags = jnp.stack([lax.axis_index("row") % 2, lax.axis_index("col") % 2]).astype(jnp.int32)
    prods = (prod_a, prod_b, prod_c)
    far_place = permute(a_place, lambda r, c: (r, c + AHEAD))
    outgoing = fill(lax.axis_size("col"), a_pick, b_pick, (*prods, flags), a_blocks, b_blocks)
    outgoing, far_place, flags = together(outgoing, far_place, flags)
    arrived = lax.all_to_all(outgoing, ("row", "col"), split_axis=0, concat_axis=0, tiled=True)
    up0, low3, b0 = compact(a_place, far_place, b_place, arrived)
    up0, low3, b0, flags = together(up0, low3, b0, flags)
    core1, odd = flags[0] == 1, flags[1] == 1

    up2 = permute(up0, lambda r, c: (r, c + 2))
    low1 = permute(low3, lambda r, c: (r, c - 2))
    b2 = permute(b0, lambda r, c: (r + 2, c))
    near0 = permute(b0, lambda r, c: (r ^ 1, c))
    firsts = [sum(SIZES[:i]) for i in range(len(SIZES))]
    last = len(SIZES) - 1
    cross = []
    for first, size in zip(firsts, SIZES):
        rows = slice(first, first + size)
        cross.append((jnp.where(odd, up0[rows], up2[rows]), jnp.where(odd, low1[rows], low3[rows])))
    cross = [jnp.stack(pair) for pair in cross[:last]] + [*cross[last]]
    *cross, b0, b2, near0 = together(*cross, b0, b2, near0)

    def over(part):
        return permute(part, lambda r, c: (r, c ^ 1))

    mid = [over(part) for part in cross[:last]]
    cross[last], cross[last + 1], mid[0] = together(cross[last], cross[last + 1], mid[0])
    mid += [over(cross[last]), over(cross[last + 1])]
    near2 = permute(b2, lambda r, c: (r ^ 1, c))
    far3 = permute(b0, lambda r, c: (r + 3, c) if r % 2 else None)
    b1, b3 = [near0, near2], [near2, far3]
    ends = []

    def onward(up1, low2):
        up3 = permute(up1, lambda r, c: (r, c + 2))
        low0 = permute(low2, lambda r, c: (r, c - 2))
        ends.append((up3, low0))

    def middle(i, up1, low2):
        first, size = firsts[i], SIZES[i]
        part = (first, size)
        return [(1, first, size, up1, (low1, part), b1), (2, first, size, (up2, part), low2, [b2])]

    def outer(i):
        first, size = firsts[i], SIZES[i]
        part = (first, size)
        return [
            (0, first, size, (up0, part), (ends[i][1], None), [b0]),
            (3, first, size, (ends[i][0], None), (low3, part), b3),
        ]

    total = None
    jobs = []
    for i in range(last):
        if i > 0:
            mid[i], total = together(mid[i], total)
        onward(mid[i][0], mid[i][1])
        size = SIZES[i]
        jobs = middle(i, (mid[i], (0, 0, size)), (mid[i], (1, 0, size))) + jobs
        total = products(flags, prods, jobs, total)
        jobs = outer(i)
    mid[last], mid[last + 1], total = together(mid[last], mid[last + 1], total)
    onward(mid[last], mid[last + 1])
    jobs = middle(last, (mid[last], None), (mid[last + 1], None)) + jobs
    total = products(flags, prods, jobs, total)
    return last_products(flags, prods, outer(last), total)


def solution(mesh):
    placed = (
        P(("row", "col"), None, None),
        P(("row", "col")),
        P(("row", "col")),
        P(("row", "col"), None, None),
        P(("row", "col")),
        P(("row", "col")),
        P(None, ("row", "col")),
        P(None, ("row", "col")),
        P(None, ("row", "col")),
    )
    return jax.shard_map(
        local, mesh=mesh, in_specs=placed, out_specs=P(("row", "col"), None, None), check_vma=False
    )
```

```python
import functools

import jax
import jax.numpy as jnp
from jax import lax
from jax.experimental import pallas as pl
from jax.experimental.pallas import tpu as pltpu
from jax.sharding import PartitionSpec as P

CBLK = 64
AHEAD = 3
PIECES = 4
SIZES = (20, 20, 16)
GROUP = 4
VMEM_LIMIT = 60 * 1024 * 1024

ANY = pl.BlockSpec(memory_space=pl.ANY)
HBM = pl.BlockSpec(memory_space=pltpu.HBM)
SMEM = pl.BlockSpec(memory_space=pltpu.SMEM)


def permute(array, mapping):
    rows, cols = lax.axis_size("row"), lax.axis_size("col")
    pairs = []
    for r in range(rows):
        for c in range(cols):
            source = mapping(r, c)
            if source is not None:
                pairs.append(((source[0] % rows) * cols + source[1] % cols, r * cols + c))
    return lax.ppermute(array, ("row", "col"), pairs)


def fill_kernel(cols, a_pick, b_pick, near_a, near_b, near_c, flags, a_blocks, b_blocks, out, a_ref, b_ref, sem):
    panel = a_blocks.shape[0]
    half = a_blocks.shape[1] // 2
    load_a = pltpu.make_async_copy(a_blocks, a_ref, sem.at[0])
    load_b = pltpu.make_async_copy(b_blocks, b_ref, sem.at[1])
    load_a.start()
    load_b.start()
    upper, lower = pl.ds(0, half), pl.ds(half, half)

    def fill_a(q, carry):
        p = a_pick[q]
        col = lax.rem(q, cols)
        behind = q - col + lax.rem(col + cols - AHEAD, cols)

        @pl.when(p < panel)
        def _():
            pltpu.make_async_copy(a_ref.at[p, upper], out.at[q, 0, upper], sem.at[2]).start()
            pltpu.make_async_copy(a_ref.at[p, lower], out.at[behind, 0, lower], sem.at[2]).start()

        return carry

    def fill_b(q, carry):
        p = b_pick[q]

        @pl.when(p < panel)
        def _():
            pltpu.make_async_copy(b_ref.at[p], out.at[q, 1], sem.at[3]).start()

        return carry

    load_a.wait()
    lax.fori_loop(0, a_pick.shape[0], fill_a, 0)
    load_b.wait()
    lax.fori_loop(0, b_pick.shape[0], fill_b, 0)
    pltpu.make_async_copy(a_blocks, a_ref, sem.at[2]).wait()
    pltpu.make_async_copy(b_blocks, b_ref, sem.at[3]).wait()


def fill(cols, a_pick, b_pick, small, a_blocks, b_blocks):
    slots = a_pick.shape[0]
    panel, width, _ = a_blocks.shape
    return pl.pallas_call(
        functools.partial(fill_kernel, cols),
        out_shape=jax.ShapeDtypeStruct((slots, 2, width, width), jnp.float32),
        in_specs=[SMEM] * 6 + [HBM, HBM],
        out_specs=HBM,
        scratch_shapes=[
            pltpu.VMEM((panel, width, width), jnp.float32),
            pltpu.VMEM((panel, width, width), jnp.float32),
            pltpu.SemaphoreType.DMA((4,)),
        ],
        compiler_params=pltpu.CompilerParams(vmem_limit_bytes=VMEM_LIMIT),
        cost_estimate=pl.CostEstimate(flops=0, bytes_accessed=16 * a_blocks.size, transcendentals=0),
        name="fill",
    )(a_pick, b_pick, *small, a_blocks, b_blocks)


def compact_kernel(parts, *refs):
    number = len(parts)
    places, arrived, outs, held = refs[:number], refs[number], refs[number + 1 : 2 * number + 1], refs[2 * number + 1 :]
    in_sem, out_sem = held[number:]
    pieces = [(n, k) for n in range(number) for k in range(PIECES)]
    for n, k in pieces:
        side, first, size = parts[n]
        step = places[n].shape[0] // PIECES

        def body(j, carry, n=n, k=k, side=side, rows=pl.ds(first, size)):
            source = arrived.at[places[n][j], side, rows]
            pltpu.make_async_copy(source, held[n].at[j], in_sem.at[n, k]).start()
            return carry

        lax.fori_loop(k * step, (k + 1) * step, body, 0, unroll=2)
    copies = []
    for n, k in pieces:
        step = places[n].shape[0] // PIECES
        piece = held[n].at[pl.ds(k * step, step)]
        copies.append(pltpu.make_async_copy(piece, outs[n].at[pl.ds(k * step, step)], out_sem.at[n, k]))
        pltpu.make_async_copy(piece, piece, in_sem.at[n, k]).wait()
        copies[-1].start()
    for copy in copies:
        copy.wait()


def compact(places, parts, arrived):
    width = arrived.shape[-1]
    shapes = [(place.shape[0], size, width) for place, (_, _, size) in zip(places, parts)]
    return pl.pallas_call(
        functools.partial(compact_kernel, tuple(parts)),
        out_shape=[jax.ShapeDtypeStruct(shape, jnp.float32) for shape in shapes],
        in_specs=[SMEM] * len(parts) + [HBM],
        out_specs=[HBM] * len(parts),
        scratch_shapes=[pltpu.VMEM(shape, jnp.float32) for shape in shapes]
        + [pltpu.SemaphoreType.DMA((len(parts), PIECES)), pltpu.SemaphoreType.DMA((len(parts), PIECES))],
        compiler_params=pltpu.CompilerParams(vmem_limit_bytes=VMEM_LIMIT),
        cost_estimate=pl.CostEstimate(flops=10**11, bytes_accessed=16 * 2**20, transcendentals=0),
        name="compact",
    )(*places, arrived)


def split(value):
    high = value.astype(jnp.bfloat16)
    low = (value - high.astype(jnp.float32)).astype(jnp.bfloat16)
    return high, low


def block_product(left, right):
    lh, ll = split(left)
    rh, rl = split(right)
    width = right.shape[1]
    wide = jnp.dot(
        jnp.concatenate([lh, ll], axis=1),
        jnp.concatenate(
            [jnp.concatenate([rh, rl], axis=1), jnp.concatenate([rh, jnp.zeros_like(rl)], axis=1)], axis=0
        ),
        preferred_element_type=jnp.float32,
    )
    return wide[:, :width] + wide[:, width:]


def rows_of(ref, spec):
    if spec is None:
        return ref
    if len(spec) == 3:
        return ref.at[spec[0], pl.ds(spec[1], spec[2])]
    return ref.at[pl.ds(spec[0], spec[1])]


def products_kernel(jobs, has_c, flags, index_a, index_b, index_c, *refs):
    refs, scratch = refs[: len(refs) - len(jobs) * 2 - 3], refs[len(refs) - len(jobs) * 2 - 3 :]
    held = [(scratch[2 * n], scratch[2 * n + 1]) for n in range(len(jobs))]
    c_ref, live, sem = scratch[2 * len(jobs) :]
    c_out = refs[-1]
    blocks = c_out.shape[0]
    entries = index_a.shape[1]
    half = c_ref.shape[1] // 2

    if has_c:
        load_c = pltpu.make_async_copy(refs[-2], c_ref, sem.at[len(jobs), 0])
        load_c.start()
    waits = []
    for n, (_, _, _, upper, lower, b) in enumerate(jobs):
        a_ref, b_ref = held[n]
        copies = [
            pltpu.make_async_copy(rows_of(refs[upper[0]], upper[1]), a_ref.at[:, pl.ds(0, half)], sem.at[n, 0]),
            pltpu.make_async_copy(rows_of(refs[lower[0]], lower[1]), a_ref.at[:, pl.ds(half, half)], sem.at[n, 1]),
        ]
        for copy in copies:
            copy.start()
        for k, source in enumerate(b):
            copy = pltpu.make_async_copy(refs[source], b_ref, sem.at[n, 2])
            if len(b) == 1:
                copy.start()
            else:
                pl.when(flags[0] == k)(copy.start)
        waits.append([*copies, copy])

    counts = []
    for n, (t, first, size, _, _, _) in enumerate(jobs):

        def listing(e, count, n=n, t=t, first=first, size=size):
            live[n, count] = e
            slot = index_a[t, e]
            used = (index_c[t, e] < blocks) & (slot >= first) & (slot < first + size)
            return count + jnp.where(used, 1, 0)

        counts.append(lax.fori_loop(0, entries, listing, 0, unroll=4))
    if has_c:
        load_c.wait()
    else:
        c_ref[...] = jnp.zeros_like(c_ref)

    for n, (t, first, _, _, _, _) in enumerate(jobs):
        a_ref, b_ref = held[n]
        for copy in waits[n]:
            copy.wait()

        def add(at, n=n, t=t, first=first, a_ref=a_ref, b_ref=b_ref):
            e = live[n, at]
            c_ref[index_c[t, e]] += block_product(a_ref[index_a[t, e] - first], b_ref[index_b[t, e]])

        def several(g, carry, add=add):
            for u in range(GROUP):
                add(g * GROUP + u)
            return carry

        def single(at, carry, add=add):
            add(at)
            return carry

        groups = counts[n] // GROUP
        lax.fori_loop(0, groups, several, 0)
        lax.fori_loop(groups * GROUP, counts[n], single, 0)
    out = pltpu.make_async_copy(c_ref, c_out, sem.at[len(jobs), 0])
    out.start()
    out.wait()


def products(flags, prods, jobs, total):
    entries = prods[0].shape[1]
    width = jobs[0][5][0].shape[1]
    has_c = total is not None
    arrays = []

    def number(array):
        for n, known in enumerate(arrays):
            if known is array:
                return n
        arrays.append(array)
        return len(arrays) - 1

    static = []
    scratch = []
    for t, first, size, upper, lower, b in jobs:
        static.append((t, first, size, (number(upper[0]), upper[1]), (number(lower[0]), lower[1]), tuple(number(x) for x in b)))
        scratch.append(pltpu.VMEM((size, width, width), jnp.float32))
        scratch.append(pltpu.VMEM(b[0].shape, jnp.float32))
    operands = [flags, *prods, *arrays]
    aliases = {}
    if has_c:
        aliases = {len(operands): 0}
        operands.append(total)
    return pl.pallas_call(
        functools.partial(products_kernel, tuple(static), has_c),
        out_shape=jax.ShapeDtypeStruct((CBLK, width, width), jnp.float32),
        in_specs=[SMEM] * 4 + [ANY] * (len(operands) - 4),
        out_specs=ANY,
        scratch_shapes=scratch
        + [
            pltpu.VMEM((CBLK, width, width), jnp.float32),
            pltpu.SMEM((len(jobs), entries + 1), jnp.int32),
            pltpu.SemaphoreType.DMA((len(jobs) + 1, 3)),
        ],
        input_output_aliases=aliases,
        compiler_params=pltpu.CompilerParams(vmem_limit_bytes=VMEM_LIMIT),
        cost_estimate=pl.CostEstimate(
            flops=6000 * entries * width**3, bytes_accessed=8 * CBLK * width * width, transcendentals=0
        ),
        name="products",
    )(*operands)


def plan_kernel(ranges, index_a, index_b, index_c, plan):
    blocks = CBLK
    entries = index_a.shape[1]

    def clear(m, carry):
        plan[4, m] = -1
        return carry

    lax.fori_loop(0, blocks, clear, 0, unroll=8)
    counts = (0, 0)
    for n, (t, first, size) in enumerate(ranges):

        def note(e, counts, t=t, first=first, size=size):
            slot, m = index_a[t, e] - first, index_c[t, e]
            used = (m < blocks) & (slot >= 0) & (slot < size)
            count, kept = counts
            new = used & (plan[4, jnp.minimum(m, blocks - 1)] < 0)

            @pl.when(new)
            def _():
                plan[4, m] = kept
                plan[3, kept] = m

            @pl.when(used)
            def _():
                plan[0, count] = slot
                plan[1, count] = index_b[t, e]
                plan[2, count] = plan[4, m]

            return count + jnp.where(used, 1, 0), kept + jnp.where(new, 1, 0)

        counts = lax.fori_loop(0, entries, note, counts)
        plan[5, n] = counts[0]
    plan[5, len(ranges)] = counts[1]


def make_plan(prods, ranges):
    entries = prods[0].shape[1]
    return pl.pallas_call(
        functools.partial(plan_kernel, tuple(ranges)),
        out_shape=jax.ShapeDtypeStruct((6, max(len(ranges) * entries, CBLK)), jnp.int32),
        in_specs=[SMEM] * 3,
        out_specs=SMEM,
        name="plan",
    )(*prods)


def last_kernel(jobs, flags, plan, *refs):
    number = len(jobs)
    c_in, c_out, b_ref, c_ref, sem = refs[len(refs) - number - 5 : len(refs) - number - 3] + refs[len(refs) - 3 :]
    held = refs[len(refs) - number - 3 : len(refs) - 3]
    half = c_ref.shape[1] // 2
    kept = plan[5, number]

    copies = []
    for n, (upper, lower, _) in enumerate(jobs):
        for part, (source, spec) in enumerate((upper, lower)):
            rows = held[n].at[:, pl.ds(part * half, half)]
            copies.append(pltpu.make_async_copy(rows_of(refs[source], spec), rows, sem.at[2 + 2 * n + part]))
    for copy in copies:
        copy.start()

    begin = 0
    for n, (_, _, b) in enumerate(jobs):
        end = plan[5, n]

        def fetch(at, carry, b=b):
            for k, source in enumerate(b):
                copy = pltpu.make_async_copy(refs[source].at[plan[1, at]], b_ref.at[at], sem.at[0])
                if len(b) == 1:
                    copy.start()
                else:
                    pl.when(flags[0] == k)(copy.start)
            return carry

        lax.fori_loop(begin, end, fetch, 0)
        begin = end

    def fetch_c(k, carry):
        pltpu.make_async_copy(c_in.at[plan[3, k]], c_ref.at[k], sem.at[0]).start()
        return carry

    lax.fori_loop(0, kept, fetch_c, 0)

    def arrive(_, carry):
        pltpu.make_async_copy(c_in.at[0], c_ref.at[0], sem.at[0]).wait()
        return carry

    lax.fori_loop(0, begin + kept, arrive, 0)
    for copy in copies:
        copy.wait()

    begin = 0
    for n in range(number):
        end = plan[5, n]

        def add(at, a_ref=held[n]):
            c_ref[plan[2, at]] += block_product(a_ref[plan[0, at]], b_ref[at])

        def several(g, carry, begin=begin, add=add):
            for u in range(GROUP):
                add(begin + g * GROUP + u)
            return carry

        def single(at, carry, add=add):
            add(at)
            return carry

        groups = (end - begin) // GROUP
        lax.fori_loop(0, groups, several, 0)
        lax.fori_loop(begin + groups * GROUP, end, single, 0)
        begin = end

    def store(k, carry):
        pltpu.make_async_copy(c_ref.at[k], c_out.at[plan[3, k]], sem.at[1]).start()
        return carry

    lax.fori_loop(0, kept, store, 0)

    def leave(_, carry):
        pltpu.make_async_copy(c_ref.at[0], c_out.at[0], sem.at[1]).wait()
        return carry

    lax.fori_loop(0, kept, leave, 0)


def last_products(flags, plan, entries, jobs, total):
    block = total.shape[1:]
    arrays = []
    static = []
    for _, _, size, upper, lower, b in jobs:
        n = len(arrays)
        arrays += [upper[0], lower[0], *b]
        static.append(((n, upper[1]), (n + 1, lower[1]), tuple(range(n + 2, len(arrays)))))
    operands = [flags, plan, *arrays, total]
    return pl.pallas_call(
        functools.partial(last_kernel, tuple(static)),
        out_shape=jax.ShapeDtypeStruct(total.shape, jnp.float32),
        in_specs=[SMEM] * 2 + [ANY] * (len(operands) - 2),
        out_specs=ANY,
        scratch_shapes=[pltpu.VMEM((size, *block), jnp.float32) for _, _, size, _, _, _ in jobs]
        + [
            pltpu.VMEM((len(jobs) * entries, *block), jnp.float32),
            pltpu.VMEM(total.shape, jnp.float32),
            pltpu.SemaphoreType.DMA((2 + 2 * len(jobs),)),
        ],
        input_output_aliases={len(operands) - 1: 0},
        compiler_params=pltpu.CompilerParams(vmem_limit_bytes=VMEM_LIMIT),
        cost_estimate=pl.CostEstimate(
            flops=6000 * entries * block[0] ** 3, bytes_accessed=8 * total.size, transcendentals=0
        ),
        name="last_products",
    )(*operands)


def together(*values):
    return lax.optimization_barrier(values)


def local(a_blocks, a_pick, a_place, b_blocks, b_pick, b_place, prod_a, prod_b, prod_c):
    flags = jnp.stack([lax.axis_index("row") % 2, lax.axis_index("col") % 2]).astype(jnp.int32)
    prods = (prod_a, prod_b, prod_c)
    far_place = permute(a_place, lambda r, c: (r, c + AHEAD))
    outgoing = fill(lax.axis_size("col"), a_pick, b_pick, (*prods, flags), a_blocks, b_blocks)
    outgoing, far_place, flags = together(outgoing, far_place, flags)
    arrived = lax.all_to_all(outgoing, ("row", "col"), split_axis=0, concat_axis=0, tiled=True)
    width = arrived.shape[-1]
    half = width // 2
    (b0,) = compact([b_place], [(1, 0, width)], arrived)
    arrived, b0 = together(arrived, b0)
    up0, low3 = compact([a_place, far_place], [(0, 0, half), (0, half, half)], arrived)
    up0, low3, flags = together(up0, low3, flags)
    core1, odd = flags[0] == 1, flags[1] == 1

    up2 = permute(up0, lambda r, c: (r, c + 2))
    low1 = permute(low3, lambda r, c: (r, c - 2))
    b2 = permute(b0, lambda r, c: (r + 2, c))
    near0 = permute(b0, lambda r, c: (r ^ 1, c))
    firsts = [sum(SIZES[:i]) for i in range(len(SIZES))]
    last = len(SIZES) - 1
    cross = []
    for first, size in zip(firsts, SIZES):
        rows = slice(first, first + size)
        cross.append((jnp.where(odd, up0[rows], up2[rows]), jnp.where(odd, low1[rows], low3[rows])))
    cross = [jnp.stack(pair) for pair in cross[:last]] + [*cross[last]]
    plan = make_plan(prods, [(t, firsts[last], SIZES[last]) for t in (0, 3)])
    *cross, b0, b2, near0, plan = together(*cross, b0, b2, near0, plan)

    def over(part):
        return permute(part, lambda r, c: (r, c ^ 1))

    mid = [over(part) for part in cross[:last]]
    cross[last], cross[last + 1], mid[0] = together(cross[last], cross[last + 1], mid[0])
    mid += [over(cross[last]), over(cross[last + 1])]
    near2 = permute(b2, lambda r, c: (r ^ 1, c))
    far3 = permute(b0, lambda r, c: (r + 3, c) if r % 2 else None)
    b1, b3 = [near0, near2], [near2, far3]
    ends = []

    def onward(up1, low2):
        up3 = permute(up1, lambda r, c: (r, c + 2))
        low0 = permute(low2, lambda r, c: (r, c - 2))
        ends.append((up3, low0))

    def middle(i, up1, low2):
        first, size = firsts[i], SIZES[i]
        part = (first, size)
        return [(1, first, size, up1, (low1, part), b1), (2, first, size, (up2, part), low2, [b2])]

    def outer(i):
        first, size = firsts[i], SIZES[i]
        part = (first, size)
        return [
            (0, first, size, (up0, part), (ends[i][1], None), [b0]),
            (3, first, size, (ends[i][0], None), (low3, part), b3),
        ]

    total = None
    jobs = []
    for i in range(last):
        if i > 0:
            mid[i], total = together(mid[i], total)
        onward(mid[i][0], mid[i][1])
        size = SIZES[i]
        jobs = middle(i, (mid[i], (0, 0, size)), (mid[i], (1, 0, size))) + jobs
        total = products(flags, prods, jobs, total)
        jobs = outer(i)
    mid[last], mid[last + 1], total = together(mid[last], mid[last + 1], total)
    onward(mid[last], mid[last + 1])
    jobs = middle(last, (mid[last], None), (mid[last + 1], None)) + jobs
    total = products(flags, prods, jobs, total)
    return last_products(flags, plan, prod_a.shape[1], outer(last), total)


def solution(mesh):
    placed = (
        P(("row", "col"), None, None),
        P(("row", "col")),
        P(("row", "col")),
        P(("row", "col"), None, None),
        P(("row", "col")),
        P(("row", "col")),
        P(None, ("row", "col")),
        P(None, ("row", "col")),
        P(None, ("row", "col")),
    )
    return jax.shard_map(
        local, mesh=mesh, in_specs=placed, out_specs=P(("row", "col"), None, None), check_vma=False
    )
```

```python
import functools

import jax
import jax.numpy as jnp
from jax import lax
from jax.experimental import pallas as pl
from jax.experimental.pallas import tpu as pltpu
from jax.sharding import PartitionSpec as P

CBLK = 64
AHEAD = 3
PIECES = 4
SIZES = (20, 20, 16)
GROUP = 4
VMEM_LIMIT = 60 * 1024 * 1024

ANY = pl.BlockSpec(memory_space=pl.ANY)
HBM = pl.BlockSpec(memory_space=pltpu.HBM)
SMEM = pl.BlockSpec(memory_space=pltpu.SMEM)


def permute(array, mapping):
    rows, cols = lax.axis_size("row"), lax.axis_size("col")
    pairs = []
    for r in range(rows):
        for c in range(cols):
            source = mapping(r, c)
            if source is not None:
                pairs.append(((source[0] % rows) * cols + source[1] % cols, r * cols + c))
    return lax.ppermute(array, ("row", "col"), pairs)


def fill_kernel(cols, a_pick, b_pick, near_a, near_b, near_c, flags, a_blocks, b_blocks, out, a_ref, b_ref, sem):
    panel = a_blocks.shape[0]
    half = a_blocks.shape[1] // 2
    load_a = pltpu.make_async_copy(a_blocks, a_ref, sem.at[0])
    load_b = pltpu.make_async_copy(b_blocks, b_ref, sem.at[1])
    load_a.start()
    load_b.start()
    upper, lower = pl.ds(0, half), pl.ds(half, half)

    def fill_a(q, carry):
        p = a_pick[q]
        col = lax.rem(q, cols)
        behind = q - col + lax.rem(col + cols - AHEAD, cols)

        @pl.when(p < panel)
        def _():
            pltpu.make_async_copy(a_ref.at[p, upper], out.at[q, 0, upper], sem.at[2]).start()
            pltpu.make_async_copy(a_ref.at[p, lower], out.at[behind, 0, lower], sem.at[2]).start()

        return carry

    def fill_b(q, carry):
        p = b_pick[q]

        @pl.when(p < panel)
        def _():
            pltpu.make_async_copy(b_ref.at[p], out.at[q, 1], sem.at[3]).start()

        return carry

    load_a.wait()
    lax.fori_loop(0, a_pick.shape[0], fill_a, 0)
    load_b.wait()
    lax.fori_loop(0, b_pick.shape[0], fill_b, 0)
    pltpu.make_async_copy(a_blocks, a_ref, sem.at[2]).wait()
    pltpu.make_async_copy(b_blocks, b_ref, sem.at[3]).wait()


def fill(cols, a_pick, b_pick, small, a_blocks, b_blocks):
    slots = a_pick.shape[0]
    panel, width, _ = a_blocks.shape
    return pl.pallas_call(
        functools.partial(fill_kernel, cols),
        out_shape=jax.ShapeDtypeStruct((slots, 2, width, width), jnp.float32),
        in_specs=[SMEM] * 6 + [HBM, HBM],
        out_specs=HBM,
        scratch_shapes=[
            pltpu.VMEM((panel, width, width), jnp.float32),
            pltpu.VMEM((panel, width, width), jnp.float32),
            pltpu.SemaphoreType.DMA((4,)),
        ],
        compiler_params=pltpu.CompilerParams(vmem_limit_bytes=VMEM_LIMIT),
        cost_estimate=pl.CostEstimate(flops=0, bytes_accessed=16 * a_blocks.size, transcendentals=0),
        name="fill",
    )(a_pick, b_pick, *small, a_blocks, b_blocks)


def compact_kernel(parts, *refs):
    number = len(parts)
    places, arrived, outs, held = refs[:number], refs[number], refs[number + 1 : 2 * number + 1], refs[2 * number + 1 :]
    in_sem, out_sem = held[number:]
    pieces = [(n, k) for n in range(number) for k in range(PIECES)]
    for n, k in pieces:
        side, first, size = parts[n]
        step = places[n].shape[0] // PIECES

        def body(j, carry, n=n, k=k, side=side, rows=pl.ds(first, size)):
            source = arrived.at[places[n][j], side, rows]
            pltpu.make_async_copy(source, held[n].at[j], in_sem.at[n, k]).start()
            return carry

        lax.fori_loop(k * step, (k + 1) * step, body, 0, unroll=2)
    copies = []
    for n, k in pieces:
        step = places[n].shape[0] // PIECES
        piece = held[n].at[pl.ds(k * step, step)]
        copies.append(pltpu.make_async_copy(piece, outs[n].at[pl.ds(k * step, step)], out_sem.at[n, k]))
        pltpu.make_async_copy(piece, piece, in_sem.at[n, k]).wait()
        copies[-1].start()
    for copy in copies:
        copy.wait()


def compact(places, parts, arrived):
    width = arrived.shape[-1]
    shapes = [(place.shape[0], size, width) for place, (_, _, size) in zip(places, parts)]
    return pl.pallas_call(
        functools.partial(compact_kernel, tuple(parts)),
        out_shape=[jax.ShapeDtypeStruct(shape, jnp.float32) for shape in shapes],
        in_specs=[SMEM] * len(parts) + [HBM],
        out_specs=[HBM] * len(parts),
        scratch_shapes=[pltpu.VMEM(shape, jnp.float32) for shape in shapes]
        + [pltpu.SemaphoreType.DMA((len(parts), PIECES)), pltpu.SemaphoreType.DMA((len(parts), PIECES))],
        compiler_params=pltpu.CompilerParams(vmem_limit_bytes=VMEM_LIMIT),
        cost_estimate=pl.CostEstimate(flops=10**11, bytes_accessed=16 * 2**20, transcendentals=0),
        name="compact",
    )(*places, arrived)


def split(value):
    high = value.astype(jnp.bfloat16)
    low = (value - high.astype(jnp.float32)).astype(jnp.bfloat16)
    return high, low


def block_product(left, right):
    lh, ll = split(left)
    rh, rl = split(right)
    width = right.shape[1]
    wide = jnp.dot(
        jnp.concatenate([lh, ll], axis=1),
        jnp.concatenate(
            [jnp.concatenate([rh, rl], axis=1), jnp.concatenate([rh, jnp.zeros_like(rl)], axis=1)], axis=0
        ),
        preferred_element_type=jnp.float32,
    )
    return wide[:, :width] + wide[:, width:]


def rows_of(ref, spec):
    if spec is None:
        return ref
    if len(spec) == 3:
        return ref.at[spec[0], pl.ds(spec[1], spec[2])]
    return ref.at[pl.ds(spec[0], spec[1])]


def products_kernel(jobs, has_c, flags, index_a, index_b, index_c, *refs):
    refs, scratch = refs[: len(refs) - len(jobs) * 2 - 3], refs[len(refs) - len(jobs) * 2 - 3 :]
    held = [(scratch[2 * n], scratch[2 * n + 1]) for n in range(len(jobs))]
    c_ref, live, sem = scratch[2 * len(jobs) :]
    c_out = refs[-1]
    blocks = c_out.shape[0]
    entries = index_a.shape[1]
    half = c_ref.shape[1] // 2

    if has_c:
        load_c = pltpu.make_async_copy(refs[-2], c_ref, sem.at[len(jobs), 0])
        load_c.start()
    waits = []
    for n, (_, _, _, upper, lower, b) in enumerate(jobs):
        a_ref, b_ref = held[n]
        copies = [
            pltpu.make_async_copy(rows_of(refs[upper[0]], upper[1]), a_ref.at[:, pl.ds(0, half)], sem.at[n, 0]),
            pltpu.make_async_copy(rows_of(refs[lower[0]], lower[1]), a_ref.at[:, pl.ds(half, half)], sem.at[n, 1]),
        ]
        for copy in copies:
            copy.start()
        for k, source in enumerate(b):
            copy = pltpu.make_async_copy(refs[source], b_ref, sem.at[n, 2])
            if len(b) == 1:
                copy.start()
            else:
                pl.when(flags[0] == k)(copy.start)
        waits.append([*copies, copy])

    counts = []
    for n, (t, first, size, _, _, _) in enumerate(jobs):

        def listing(e, count, n=n, t=t, first=first, size=size):
            live[n, count] = e
            slot = index_a[t, e]
            used = (index_c[t, e] < blocks) & (slot >= first) & (slot < first + size)
            return count + jnp.where(used, 1, 0)

        counts.append(lax.fori_loop(0, entries, listing, 0, unroll=4))
    if has_c:
        load_c.wait()
    else:
        c_ref[...] = jnp.zeros_like(c_ref)

    for n, (t, first, _, _, _, _) in enumerate(jobs):
        a_ref, b_ref = held[n]
        for copy in waits[n]:
            copy.wait()

        def add(at, n=n, t=t, first=first, a_ref=a_ref, b_ref=b_ref):
            e = live[n, at]
            c_ref[index_c[t, e]] += block_product(a_ref[index_a[t, e] - first], b_ref[index_b[t, e]])

        def product(at, n=n, t=t, first=first, a_ref=a_ref, b_ref=b_ref):
            e = live[n, at]
            return index_c[t, e], block_product(a_ref[index_a[t, e] - first], b_ref[index_b[t, e]])

        def several(g, carry, product=product):
            for m, value in [product(g * GROUP + u) for u in range(GROUP)]:
                c_ref[m] += value
            return carry

        def single(at, carry, add=add):
            add(at)
            return carry

        groups = counts[n] // GROUP
        lax.fori_loop(0, groups, several, 0)
        lax.fori_loop(groups * GROUP, counts[n], single, 0)
    out = pltpu.make_async_copy(c_ref, c_out, sem.at[len(jobs), 0])
    out.start()
    out.wait()


def products(flags, prods, jobs, total):
    entries = prods[0].shape[1]
    width = jobs[0][5][0].shape[1]
    has_c = total is not None
    arrays = []

    def number(array):
        for n, known in enumerate(arrays):
            if known is array:
                return n
        arrays.append(array)
        return len(arrays) - 1

    static = []
    scratch = []
    for t, first, size, upper, lower, b in jobs:
        static.append((t, first, size, (number(upper[0]), upper[1]), (number(lower[0]), lower[1]), tuple(number(x) for x in b)))
        scratch.append(pltpu.VMEM((size, width, width), jnp.float32))
        scratch.append(pltpu.VMEM(b[0].shape, jnp.float32))
    operands = [flags, *prods, *arrays]
    aliases = {}
    if has_c:
        aliases = {len(operands): 0}
        operands.append(total)
    return pl.pallas_call(
        functools.partial(products_kernel, tuple(static), has_c),
        out_shape=jax.ShapeDtypeStruct((CBLK, width, width), jnp.float32),
        in_specs=[SMEM] * 4 + [ANY] * (len(operands) - 4),
        out_specs=ANY,
        scratch_shapes=scratch
        + [
            pltpu.VMEM((CBLK, width, width), jnp.float32),
            pltpu.SMEM((len(jobs), entries + 1), jnp.int32),
            pltpu.SemaphoreType.DMA((len(jobs) + 1, 3)),
        ],
        input_output_aliases=aliases,
        compiler_params=pltpu.CompilerParams(vmem_limit_bytes=VMEM_LIMIT),
        cost_estimate=pl.CostEstimate(
            flops=6000 * entries * width**3, bytes_accessed=8 * CBLK * width * width, transcendentals=0
        ),
        name="products",
    )(*operands)


def plan_kernel(ranges, index_a, index_b, index_c, plan):
    blocks = CBLK
    entries = index_a.shape[1]

    def clear(m, carry):
        plan[4, m] = -1
        return carry

    lax.fori_loop(0, blocks, clear, 0, unroll=8)
    counts = (0, 0)
    for n, (t, first, size) in enumerate(ranges):

        def note(e, counts, t=t, first=first, size=size):
            slot, m = index_a[t, e] - first, index_c[t, e]
            used = (m < blocks) & (slot >= 0) & (slot < size)
            count, kept = counts
            new = used & (plan[4, jnp.minimum(m, blocks - 1)] < 0)

            @pl.when(new)
            def _():
                plan[4, m] = kept
                plan[3, kept] = m

            @pl.when(used)
            def _():
                plan[0, count] = slot
                plan[1, count] = index_b[t, e]
                plan[2, count] = plan[4, m]

            return count + jnp.where(used, 1, 0), kept + jnp.where(new, 1, 0)

        counts = lax.fori_loop(0, entries, note, counts)
        plan[5, n] = counts[0]
    plan[5, len(ranges)] = counts[1]


def make_plan(prods, ranges):
    entries = prods[0].shape[1]
    return pl.pallas_call(
        functools.partial(plan_kernel, tuple(ranges)),
        out_shape=jax.ShapeDtypeStruct((6, max(len(ranges) * entries, CBLK)), jnp.int32),
        in_specs=[SMEM] * 3,
        out_specs=SMEM,
        name="plan",
    )(*prods)


def last_kernel(jobs, flags, plan, *refs):
    number = len(jobs)
    c_in, c_out, b_ref, c_ref, sem = refs[len(refs) - number - 5 : len(refs) - number - 3] + refs[len(refs) - 3 :]
    held = refs[len(refs) - number - 3 : len(refs) - 3]
    half = c_ref.shape[1] // 2
    kept = plan[5, number]

    copies = []
    for n, (upper, lower, _) in enumerate(jobs):
        for part, (source, spec) in enumerate((upper, lower)):
            rows = held[n].at[:, pl.ds(part * half, half)]
            copies.append(pltpu.make_async_copy(rows_of(refs[source], spec), rows, sem.at[2 + 2 * n + part]))
    for copy in copies:
        copy.start()

    begin = 0
    for n, (_, _, b) in enumerate(jobs):
        end = plan[5, n]

        def fetch(at, carry, b=b):
            for k, source in enumerate(b):
                copy = pltpu.make_async_copy(refs[source].at[plan[1, at]], b_ref.at[at], sem.at[0])
                if len(b) == 1:
                    copy.start()
                else:
                    pl.when(flags[0] == k)(copy.start)
            return carry

        lax.fori_loop(begin, end, fetch, 0)
        begin = end

    def fetch_c(k, carry):
        pltpu.make_async_copy(c_in.at[plan[3, k]], c_ref.at[k], sem.at[0]).start()
        return carry

    lax.fori_loop(0, kept, fetch_c, 0)

    def arrive(_, carry):
        pltpu.make_async_copy(c_in.at[0], c_ref.at[0], sem.at[0]).wait()
        return carry

    lax.fori_loop(0, begin + kept, arrive, 0)
    for copy in copies:
        copy.wait()

    begin = 0
    for n in range(number):
        end = plan[5, n]

        def add(at, a_ref=held[n]):
            c_ref[plan[2, at]] += block_product(a_ref[plan[0, at]], b_ref[at])

        def product(at, a_ref=held[n]):
            return plan[2, at], block_product(a_ref[plan[0, at]], b_ref[at])

        def several(g, carry, begin=begin, product=product):
            for m, value in [product(begin + g * GROUP + u) for u in range(GROUP)]:
                c_ref[m] += value
            return carry

        def single(at, carry, add=add):
            add(at)
            return carry

        groups = (end - begin) // GROUP
        lax.fori_loop(0, groups, several, 0)
        lax.fori_loop(begin + groups * GROUP, end, single, 0)
        begin = end

    def store(k, carry):
        pltpu.make_async_copy(c_ref.at[k], c_out.at[plan[3, k]], sem.at[1]).start()
        return carry

    lax.fori_loop(0, kept, store, 0)

    def leave(_, carry):
        pltpu.make_async_copy(c_ref.at[0], c_out.at[0], sem.at[1]).wait()
        return carry

    lax.fori_loop(0, kept, leave, 0)


def last_products(flags, plan, entries, jobs, total):
    block = total.shape[1:]
    arrays = []
    static = []
    for _, _, size, upper, lower, b in jobs:
        n = len(arrays)
        arrays += [upper[0], lower[0], *b]
        static.append(((n, upper[1]), (n + 1, lower[1]), tuple(range(n + 2, len(arrays)))))
    operands = [flags, plan, *arrays, total]
    return pl.pallas_call(
        functools.partial(last_kernel, tuple(static)),
        out_shape=jax.ShapeDtypeStruct(total.shape, jnp.float32),
        in_specs=[SMEM] * 2 + [ANY] * (len(operands) - 2),
        out_specs=ANY,
        scratch_shapes=[pltpu.VMEM((size, *block), jnp.float32) for _, _, size, _, _, _ in jobs]
        + [
            pltpu.VMEM((len(jobs) * entries, *block), jnp.float32),
            pltpu.VMEM(total.shape, jnp.float32),
            pltpu.SemaphoreType.DMA((2 + 2 * len(jobs),)),
        ],
        input_output_aliases={len(operands) - 1: 0},
        compiler_params=pltpu.CompilerParams(vmem_limit_bytes=VMEM_LIMIT),
        cost_estimate=pl.CostEstimate(
            flops=6000 * entries * block[0] ** 3, bytes_accessed=8 * total.size, transcendentals=0
        ),
        name="last_products",
    )(*operands)


def together(*values):
    return lax.optimization_barrier(values)


def local(a_blocks, a_pick, a_place, b_blocks, b_pick, b_place, prod_a, prod_b, prod_c):
    flags = jnp.stack([lax.axis_index("row") % 2, lax.axis_index("col") % 2]).astype(jnp.int32)
    prods = (prod_a, prod_b, prod_c)
    outgoing = fill(lax.axis_size("col"), a_pick, b_pick, (*prods, flags), a_blocks, b_blocks)
    outgoing, flags = together(outgoing, flags)
    arrived = lax.all_to_all(outgoing, ("row", "col"), split_axis=0, concat_axis=0, tiled=True)
    width = arrived.shape[-1]
    half = width // 2
    arrived, a_place = together(arrived, a_place)
    far_place = permute(a_place, lambda r, c: (r, c + AHEAD))
    (b0,) = compact([b_place], [(1, 0, width)], arrived)
    arrived, b0 = together(arrived, b0)
    (up0,) = compact([a_place], [(0, 0, half)], arrived)
    arrived, far_place, up0 = together(arrived, far_place, up0)
    (low3,) = compact([far_place], [(0, half, half)], arrived)
    up0, low3, flags = together(up0, low3, flags)
    core1, odd = flags[0] == 1, flags[1] == 1

    up2 = permute(up0, lambda r, c: (r, c + 2))
    low1 = permute(low3, lambda r, c: (r, c - 2))
    b2 = permute(b0, lambda r, c: (r + 2, c))
    near0 = permute(b0, lambda r, c: (r ^ 1, c))
    firsts = [sum(SIZES[:i]) for i in range(len(SIZES))]
    last = len(SIZES) - 1
    cross = []
    for first, size in zip(firsts, SIZES):
        rows = slice(first, first + size)
        cross.append((jnp.where(odd, up0[rows], up2[rows]), jnp.where(odd, low1[rows], low3[rows])))
    cross = [jnp.stack(pair) for pair in cross[:last]] + [*cross[last]]
    plan = make_plan(prods, [(t, firsts[last], SIZES[last]) for t in (0, 3)])
    *cross, b0, b2, near0, plan = together(*cross, b0, b2, near0, plan)

    def over(part):
        return permute(part, lambda r, c: (r, c ^ 1))

    mid = [over(part) for part in cross[:last]]
    cross[last], cross[last + 1], mid[0] = together(cross[last], cross[last + 1], mid[0])
    mid += [over(cross[last]), over(cross[last + 1])]
    near2 = permute(b2, lambda r, c: (r ^ 1, c))
    far3 = permute(b0, lambda r, c: (r + 3, c) if r % 2 else None)
    b1, b3 = [near0, near2], [near2, far3]
    ends = []

    def onward(up1, low2):
        up3 = permute(up1, lambda r, c: (r, c + 2))
        low0 = permute(low2, lambda r, c: (r, c - 2))
        ends.append((up3, low0))

    def middle(i, up1, low2):
        first, size = firsts[i], SIZES[i]
        part = (first, size)
        return [(1, first, size, up1, (low1, part), b1), (2, first, size, (up2, part), low2, [b2])]

    def outer(i):
        first, size = firsts[i], SIZES[i]
        part = (first, size)
        return [
            (0, first, size, (up0, part), (ends[i][1], None), [b0]),
            (3, first, size, (ends[i][0], None), (low3, part), b3),
        ]

    total = None
    jobs = []
    for i in range(last):
        if i > 0:
            mid[i], total = together(mid[i], total)
        onward(mid[i][0], mid[i][1])
        size = SIZES[i]
        jobs = middle(i, (mid[i], (0, 0, size)), (mid[i], (1, 0, size))) + jobs
        total = products(flags, prods, jobs, total)
        jobs = outer(i)
    mid[last], mid[last + 1], total = together(mid[last], mid[last + 1], total)
    onward(mid[last], mid[last + 1])
    jobs = middle(last, (mid[last], None), (mid[last + 1], None)) + jobs
    total = products(flags, prods, jobs, total)
    return last_products(flags, plan, prod_a.shape[1], outer(last), total)


def solution(mesh):
    placed = (
        P(("row", "col"), None, None),
        P(("row", "col")),
        P(("row", "col")),
        P(("row", "col"), None, None),
        P(("row", "col")),
        P(("row", "col")),
        P(None, ("row", "col")),
        P(None, ("row", "col")),
        P(None, ("row", "col")),
    )
    return jax.shard_map(
        local, mesh=mesh, in_specs=placed, out_specs=P(("row", "col"), None, None), check_vma=False
    )
```

```python
import functools

import jax
import jax.numpy as jnp
from jax import lax
from jax.experimental import pallas as pl
from jax.experimental.pallas import tpu as pltpu
from jax.sharding import PartitionSpec as P

CBLK = 64
AHEAD = 3
PIECES = 4
SIZES = (20, 20, 16)
GROUPS = (8, 4, 2, 1)
VMEM_LIMIT = 60 * 1024 * 1024

ANY = pl.BlockSpec(memory_space=pl.ANY)
HBM = pl.BlockSpec(memory_space=pltpu.HBM)
SMEM = pl.BlockSpec(memory_space=pltpu.SMEM)


def permute(array, mapping):
    rows, cols = lax.axis_size("row"), lax.axis_size("col")
    pairs = []
    for r in range(rows):
        for c in range(cols):
            source = mapping(r, c)
            if source is not None:
                pairs.append(((source[0] % rows) * cols + source[1] % cols, r * cols + c))
    return lax.ppermute(array, ("row", "col"), pairs)


def fill_kernel(cols, a_pick, b_pick, near_a, near_b, near_c, flags, a_blocks, b_blocks, out, a_ref, b_ref, sem):
    panel = a_blocks.shape[0]
    half = a_blocks.shape[1] // 2
    load_a = pltpu.make_async_copy(a_blocks, a_ref, sem.at[0])
    load_b = pltpu.make_async_copy(b_blocks, b_ref, sem.at[1])
    load_a.start()
    load_b.start()
    upper, lower = pl.ds(0, half), pl.ds(half, half)

    def fill_a(q, carry):
        p = a_pick[q]
        col = lax.rem(q, cols)
        behind = q - col + lax.rem(col + cols - AHEAD, cols)

        @pl.when(p < panel)
        def _():
            pltpu.make_async_copy(a_ref.at[p, upper], out.at[q, 0, upper], sem.at[2]).start()
            pltpu.make_async_copy(a_ref.at[p, lower], out.at[behind, 0, lower], sem.at[2]).start()

        return carry

    def fill_b(q, carry):
        p = b_pick[q]

        @pl.when(p < panel)
        def _():
            pltpu.make_async_copy(b_ref.at[p], out.at[q, 1], sem.at[3]).start()

        return carry

    load_a.wait()
    lax.fori_loop(0, a_pick.shape[0], fill_a, 0)
    load_b.wait()
    lax.fori_loop(0, b_pick.shape[0], fill_b, 0)
    pltpu.make_async_copy(a_blocks, a_ref, sem.at[2]).wait()
    pltpu.make_async_copy(b_blocks, b_ref, sem.at[3]).wait()


def fill(cols, a_pick, b_pick, small, a_blocks, b_blocks):
    slots = a_pick.shape[0]
    panel, width, _ = a_blocks.shape
    return pl.pallas_call(
        functools.partial(fill_kernel, cols),
        out_shape=jax.ShapeDtypeStruct((slots, 2, width, width), jnp.float32),
        in_specs=[SMEM] * 6 + [HBM, HBM],
        out_specs=HBM,
        scratch_shapes=[
            pltpu.VMEM((panel, width, width), jnp.float32),
            pltpu.VMEM((panel, width, width), jnp.float32),
            pltpu.SemaphoreType.DMA((4,)),
        ],
        compiler_params=pltpu.CompilerParams(vmem_limit_bytes=VMEM_LIMIT),
        cost_estimate=pl.CostEstimate(flops=0, bytes_accessed=16 * a_blocks.size, transcendentals=0),
        name="fill",
    )(a_pick, b_pick, *small, a_blocks, b_blocks)


def compact_kernel(parts, *refs):
    number = len(parts)
    places, arrived, outs, held = refs[:number], refs[number], refs[number + 1 : 2 * number + 1], refs[2 * number + 1 :]
    in_sem, out_sem = held[number:]
    pieces = [(n, k) for n in range(number) for k in range(PIECES)]
    for n, k in pieces:
        side, first, size = parts[n]
        step = places[n].shape[0] // PIECES

        def body(j, carry, n=n, k=k, side=side, rows=pl.ds(first, size)):
            source = arrived.at[places[n][j], side, rows]
            pltpu.make_async_copy(source, held[n].at[j], in_sem.at[n, k]).start()
            return carry

        lax.fori_loop(k * step, (k + 1) * step, body, 0, unroll=2)
    copies = []
    for n, k in pieces:
        step = places[n].shape[0] // PIECES
        piece = held[n].at[pl.ds(k * step, step)]
        copies.append(pltpu.make_async_copy(piece, outs[n].at[pl.ds(k * step, step)], out_sem.at[n, k]))
        pltpu.make_async_copy(piece, piece, in_sem.at[n, k]).wait()
        copies[-1].start()
    for copy in copies:
        copy.wait()


def compact(places, parts, arrived):
    width = arrived.shape[-1]
    shapes = [(place.shape[0], size, width) for place, (_, _, size) in zip(places, parts)]
    return pl.pallas_call(
        functools.partial(compact_kernel, tuple(parts)),
        out_shape=[jax.ShapeDtypeStruct(shape, jnp.float32) for shape in shapes],
        in_specs=[SMEM] * len(parts) + [HBM],
        out_specs=[HBM] * len(parts),
        scratch_shapes=[pltpu.VMEM(shape, jnp.float32) for shape in shapes]
        + [pltpu.SemaphoreType.DMA((len(parts), PIECES)), pltpu.SemaphoreType.DMA((len(parts), PIECES))],
        compiler_params=pltpu.CompilerParams(vmem_limit_bytes=VMEM_LIMIT),
        cost_estimate=pl.CostEstimate(flops=10**11, bytes_accessed=16 * 2**20, transcendentals=0),
        name="compact",
    )(*places, arrived)


def split(value):
    high = value.astype(jnp.bfloat16)
    low = (value - high.astype(jnp.float32)).astype(jnp.bfloat16)
    return high, low


def block_product(left, right):
    lh, ll = split(left)
    rh, rl = split(right)
    width = right.shape[1]
    wide = jnp.dot(
        jnp.concatenate([lh, ll], axis=1),
        jnp.concatenate(
            [jnp.concatenate([rh, rl], axis=1), jnp.concatenate([rh, jnp.zeros_like(rl)], axis=1)], axis=0
        ),
        preferred_element_type=jnp.float32,
    )
    return wide[:, :width] + wide[:, width:]


def add_all(c_ref, product, count):
    start = 0
    for group in GROUPS:

        def several(g, carry, group=group, start=start):
            for m, value in [product(start + g * group + u) for u in range(group)]:
                c_ref[m] += value
            return carry

        number = (count - start) // group
        lax.fori_loop(0, number, several, 0)
        start = start + number * group


def rows_of(ref, spec):
    if spec is None:
        return ref
    if len(spec) == 3:
        return ref.at[spec[0], pl.ds(spec[1], spec[2])]
    return ref.at[pl.ds(spec[0], spec[1])]


def products_kernel(jobs, has_c, flags, index_a, index_b, index_c, *refs):
    refs, scratch = refs[: len(refs) - len(jobs) * 2 - 3], refs[len(refs) - len(jobs) * 2 - 3 :]
    held = [(scratch[2 * n], scratch[2 * n + 1]) for n in range(len(jobs))]
    c_ref, live, sem = scratch[2 * len(jobs) :]
    c_out = refs[-1]
    blocks = c_out.shape[0]
    entries = index_a.shape[1]
    half = c_ref.shape[1] // 2

    if has_c:
        load_c = pltpu.make_async_copy(refs[-2], c_ref, sem.at[len(jobs), 0])
        load_c.start()
    waits = []
    for n, (_, _, _, upper, lower, b) in enumerate(jobs):
        a_ref, b_ref = held[n]
        copies = [
            pltpu.make_async_copy(rows_of(refs[upper[0]], upper[1]), a_ref.at[:, pl.ds(0, half)], sem.at[n, 0]),
            pltpu.make_async_copy(rows_of(refs[lower[0]], lower[1]), a_ref.at[:, pl.ds(half, half)], sem.at[n, 1]),
        ]
        for copy in copies:
            copy.start()
        for k, source in enumerate(b):
            copy = pltpu.make_async_copy(refs[source], b_ref, sem.at[n, 2])
            if len(b) == 1:
                copy.start()
            else:
                pl.when(flags[0] == k)(copy.start)
        waits.append([*copies, copy])

    counts = []
    for n, (t, first, size, _, _, _) in enumerate(jobs):

        def listing(e, count, n=n, t=t, first=first, size=size):
            live[n, count] = e
            slot = index_a[t, e]
            used = (index_c[t, e] < blocks) & (slot >= first) & (slot < first + size)
            return count + jnp.where(used, 1, 0)

        counts.append(lax.fori_loop(0, entries, listing, 0, unroll=4))
    if has_c:
        load_c.wait()
    else:
        c_ref[...] = jnp.zeros_like(c_ref)

    for n, (t, first, _, _, _, _) in enumerate(jobs):
        a_ref, b_ref = held[n]
        for copy in waits[n]:
            copy.wait()

        def product(at, n=n, t=t, first=first, a_ref=a_ref, b_ref=b_ref):
            e = live[n, at]
            return index_c[t, e], block_product(a_ref[index_a[t, e] - first], b_ref[index_b[t, e]])

        add_all(c_ref, product, counts[n])
    out = pltpu.make_async_copy(c_ref, c_out, sem.at[len(jobs), 0])
    out.start()
    out.wait()


def products(flags, prods, jobs, total):
    entries = prods[0].shape[1]
    width = jobs[0][5][0].shape[1]
    has_c = total is not None
    arrays = []

    def number(array):
        for n, known in enumerate(arrays):
            if known is array:
                return n
        arrays.append(array)
        return len(arrays) - 1

    static = []
    scratch = []
    for t, first, size, upper, lower, b in jobs:
        static.append((t, first, size, (number(upper[0]), upper[1]), (number(lower[0]), lower[1]), tuple(number(x) for x in b)))
        scratch.append(pltpu.VMEM((size, width, width), jnp.float32))
        scratch.append(pltpu.VMEM(b[0].shape, jnp.float32))
    operands = [flags, *prods, *arrays]
    aliases = {}
    if has_c:
        aliases = {len(operands): 0}
        operands.append(total)
    return pl.pallas_call(
        functools.partial(products_kernel, tuple(static), has_c),
        out_shape=jax.ShapeDtypeStruct((CBLK, width, width), jnp.float32),
        in_specs=[SMEM] * 4 + [ANY] * (len(operands) - 4),
        out_specs=ANY,
        scratch_shapes=scratch
        + [
            pltpu.VMEM((CBLK, width, width), jnp.float32),
            pltpu.SMEM((len(jobs), entries + 1), jnp.int32),
            pltpu.SemaphoreType.DMA((len(jobs) + 1, 3)),
        ],
        input_output_aliases=aliases,
        compiler_params=pltpu.CompilerParams(vmem_limit_bytes=VMEM_LIMIT),
        cost_estimate=pl.CostEstimate(
            flops=6000 * entries * width**3, bytes_accessed=8 * CBLK * width * width, transcendentals=0
        ),
        name="products",
    )(*operands)


def plan_kernel(ranges, index_a, index_b, index_c, plan):
    blocks = CBLK
    entries = index_a.shape[1]

    def clear(m, carry):
        plan[4, m] = -1
        return carry

    lax.fori_loop(0, blocks, clear, 0, unroll=8)
    counts = (0, 0)
    for n, (t, first, size) in enumerate(ranges):

        def note(e, counts, t=t, first=first, size=size):
            slot, m = index_a[t, e] - first, index_c[t, e]
            used = (m < blocks) & (slot >= 0) & (slot < size)
            count, kept = counts
            new = used & (plan[4, jnp.minimum(m, blocks - 1)] < 0)

            @pl.when(new)
            def _():
                plan[4, m] = kept
                plan[3, kept] = m

            @pl.when(used)
            def _():
                plan[0, count] = slot
                plan[1, count] = index_b[t, e]
                plan[2, count] = plan[4, m]

            return count + jnp.where(used, 1, 0), kept + jnp.where(new, 1, 0)

        counts = lax.fori_loop(0, entries, note, counts)
        plan[5, n] = counts[0]
    plan[5, len(ranges)] = counts[1]


def make_plan(prods, ranges):
    entries = prods[0].shape[1]
    return pl.pallas_call(
        functools.partial(plan_kernel, tuple(ranges)),
        out_shape=jax.ShapeDtypeStruct((6, max(len(ranges) * entries, CBLK)), jnp.int32),
        in_specs=[SMEM] * 3,
        out_specs=SMEM,
        name="plan",
    )(*prods)


def last_kernel(jobs, flags, plan, *refs):
    number = len(jobs)
    c_in, c_out, b_ref, c_ref, sem = refs[len(refs) - number - 5 : len(refs) - number - 3] + refs[len(refs) - 3 :]
    held = refs[len(refs) - number - 3 : len(refs) - 3]
    half = c_ref.shape[1] // 2
    kept = plan[5, number]

    copies = []
    for n, (upper, lower, _) in enumerate(jobs):
        for part, (source, spec) in enumerate((upper, lower)):
            rows = held[n].at[:, pl.ds(part * half, half)]
            copies.append(pltpu.make_async_copy(rows_of(refs[source], spec), rows, sem.at[2 + 2 * n + part]))
    for copy in copies:
        copy.start()

    begin = 0
    for n, (_, _, b) in enumerate(jobs):
        end = plan[5, n]

        def fetch(at, carry, b=b):
            for k, source in enumerate(b):
                copy = pltpu.make_async_copy(refs[source].at[plan[1, at]], b_ref.at[at], sem.at[0])
                if len(b) == 1:
                    copy.start()
                else:
                    pl.when(flags[0] == k)(copy.start)
            return carry

        lax.fori_loop(begin, end, fetch, 0)
        begin = end

    def fetch_c(k, carry):
        pltpu.make_async_copy(c_in.at[plan[3, k]], c_ref.at[k], sem.at[0]).start()
        return carry

    lax.fori_loop(0, kept, fetch_c, 0)

    def arrive(_, carry):
        pltpu.make_async_copy(c_in.at[0], c_ref.at[0], sem.at[0]).wait()
        return carry

    lax.fori_loop(0, begin + kept, arrive, 0)
    for copy in copies:
        copy.wait()

    begin = 0
    for n in range(number):
        end = plan[5, n]

        def product(at, a_ref=held[n]):
            return plan[2, at], block_product(a_ref[plan[0, at]], b_ref[at])

        add_all(c_ref, lambda at, begin=begin, product=product: product(begin + at), end - begin)
        begin = end

    def store(k, carry):
        pltpu.make_async_copy(c_ref.at[k], c_out.at[plan[3, k]], sem.at[1]).start()
        return carry

    lax.fori_loop(0, kept, store, 0)

    def leave(_, carry):
        pltpu.make_async_copy(c_ref.at[0], c_out.at[0], sem.at[1]).wait()
        return carry

    lax.fori_loop(0, kept, leave, 0)


def last_products(flags, plan, entries, jobs, total):
    block = total.shape[1:]
    arrays = []
    static = []
    for _, _, size, upper, lower, b in jobs:
        n = len(arrays)
        arrays += [upper[0], lower[0], *b]
        static.append(((n, upper[1]), (n + 1, lower[1]), tuple(range(n + 2, len(arrays)))))
    operands = [flags, plan, *arrays, total]
    return pl.pallas_call(
        functools.partial(last_kernel, tuple(static)),
        out_shape=jax.ShapeDtypeStruct(total.shape, jnp.float32),
        in_specs=[SMEM] * 2 + [ANY] * (len(operands) - 2),
        out_specs=ANY,
        scratch_shapes=[pltpu.VMEM((size, *block), jnp.float32) for _, _, size, _, _, _ in jobs]
        + [
            pltpu.VMEM((len(jobs) * entries, *block), jnp.float32),
            pltpu.VMEM(total.shape, jnp.float32),
            pltpu.SemaphoreType.DMA((2 + 2 * len(jobs),)),
        ],
        input_output_aliases={len(operands) - 1: 0},
        compiler_params=pltpu.CompilerParams(vmem_limit_bytes=VMEM_LIMIT),
        cost_estimate=pl.CostEstimate(
            flops=6000 * entries * block[0] ** 3, bytes_accessed=8 * total.size, transcendentals=0
        ),
        name="last_products",
    )(*operands)


def together(*values):
    return lax.optimization_barrier(values)


def local(a_blocks, a_pick, a_place, b_blocks, b_pick, b_place, prod_a, prod_b, prod_c):
    flags = jnp.stack([lax.axis_index("row") % 2, lax.axis_index("col") % 2]).astype(jnp.int32)
    prods = (prod_a, prod_b, prod_c)
    outgoing = fill(lax.axis_size("col"), a_pick, b_pick, (*prods, flags), a_blocks, b_blocks)
    outgoing, flags = together(outgoing, flags)
    arrived = lax.all_to_all(outgoing, ("row", "col"), split_axis=0, concat_axis=0, tiled=True)
    width = arrived.shape[-1]
    half = width // 2
    arrived, a_place = together(arrived, a_place)
    far_place = permute(a_place, lambda r, c: (r, c + AHEAD))
    (b0,) = compact([b_place], [(1, 0, width)], arrived)
    arrived, b0 = together(arrived, b0)
    (up0,) = compact([a_place], [(0, 0, half)], arrived)
    arrived, far_place, up0 = together(arrived, far_place, up0)
    (low3,) = compact([far_place], [(0, half, half)], arrived)
    up0, low3, flags = together(up0, low3, flags)
    core1, odd = flags[0] == 1, flags[1] == 1

    up2 = permute(up0, lambda r, c: (r, c + 2))
    low1 = permute(low3, lambda r, c: (r, c - 2))
    b2 = permute(b0, lambda r, c: (r + 2, c))
    near0 = permute(b0, lambda r, c: (r ^ 1, c))
    firsts = [sum(SIZES[:i]) for i in range(len(SIZES))]
    last = len(SIZES) - 1
    cross = []
    for first, size in zip(firsts, SIZES):
        rows = slice(first, first + size)
        cross.append((jnp.where(odd, up0[rows], up2[rows]), jnp.where(odd, low1[rows], low3[rows])))
    cross = [jnp.stack(pair) for pair in cross[:last]] + [*cross[last]]
    plan = make_plan(prods, [(t, firsts[last], SIZES[last]) for t in (0, 3)])
    *cross, b0, b2, near0, plan = together(*cross, b0, b2, near0, plan)

    def over(part):
        return permute(part, lambda r, c: (r, c ^ 1))

    mid = [over(part) for part in cross[:last]]
    cross[last], cross[last + 1], mid[0] = together(cross[last], cross[last + 1], mid[0])
    mid += [over(cross[last]), over(cross[last + 1])]
    near2 = permute(b2, lambda r, c: (r ^ 1, c))
    far3 = permute(b0, lambda r, c: (r + 3, c) if r % 2 else None)
    b1, b3 = [near0, near2], [near2, far3]
    ends = []

    def onward(up1, low2):
        up3 = permute(up1, lambda r, c: (r, c + 2))
        low0 = permute(low2, lambda r, c: (r, c - 2))
        ends.append((up3, low0))

    def middle(i, up1, low2):
        first, size = firsts[i], SIZES[i]
        part = (first, size)
        return [(1, first, size, up1, (low1, part), b1), (2, first, size, (up2, part), low2, [b2])]

    def outer(i):
        first, size = firsts[i], SIZES[i]
        part = (first, size)
        return [
            (0, first, size, (up0, part), (ends[i][1], None), [b0]),
            (3, first, size, (ends[i][0], None), (low3, part), b3),
        ]

    total = None
    jobs = []
    for i in range(last):
        if i > 0:
            mid[i], total = together(mid[i], total)
        onward(mid[i][0], mid[i][1])
        size = SIZES[i]
        jobs = middle(i, (mid[i], (0, 0, size)), (mid[i], (1, 0, size))) + jobs
        total = products(flags, prods, jobs, total)
        jobs = outer(i)
    mid[last], mid[last + 1], total = together(mid[last], mid[last + 1], total)
    onward(mid[last], mid[last + 1])
    jobs = middle(last, (mid[last], None), (mid[last + 1], None)) + jobs
    total = products(flags, prods, jobs, total)
    return last_products(flags, plan, prod_a.shape[1], outer(last), total)


def solution(mesh):
    placed = (
        P(("row", "col"), None, None),
        P(("row", "col")),
        P(("row", "col")),
        P(("row", "col"), None, None),
        P(("row", "col")),
        P(("row", "col")),
        P(None, ("row", "col")),
        P(None, ("row", "col")),
        P(None, ("row", "col")),
    )
    return jax.shard_map(
        local, mesh=mesh, in_specs=placed, out_specs=P(("row", "col"), None, None), check_vma=False
    )
```

```python
import functools

import jax
import jax.numpy as jnp
from jax import lax
from jax.experimental import pallas as pl
from jax.experimental.pallas import tpu as pltpu
from jax.sharding import PartitionSpec as P

CBLK = 64
AHEAD = 3
PIECES = 8
SIZES = (20, 20, 16)
GROUPS = (8, 4, 2, 1)
VMEM_LIMIT = 60 * 1024 * 1024

ANY = pl.BlockSpec(memory_space=pl.ANY)
HBM = pl.BlockSpec(memory_space=pltpu.HBM)
SMEM = pl.BlockSpec(memory_space=pltpu.SMEM)


def permute(array, mapping):
    rows, cols = lax.axis_size("row"), lax.axis_size("col")
    pairs = []
    for r in range(rows):
        for c in range(cols):
            source = mapping(r, c)
            if source is not None:
                pairs.append(((source[0] % rows) * cols + source[1] % cols, r * cols + c))
    return lax.ppermute(array, ("row", "col"), pairs)


def fill_kernel(cols, a_pick, b_pick, near_a, near_b, near_c, flags, a_blocks, b_blocks, out, a_ref, b_ref, sem):
    panel = a_blocks.shape[0]
    half = a_blocks.shape[1] // 2
    load_a = pltpu.make_async_copy(a_blocks, a_ref, sem.at[0])
    load_b = pltpu.make_async_copy(b_blocks, b_ref, sem.at[1])
    load_a.start()
    load_b.start()
    upper, lower = pl.ds(0, half), pl.ds(half, half)

    def fill_a(q, carry):
        p = a_pick[q]
        col = lax.rem(q, cols)
        behind = q - col + lax.rem(col + cols - AHEAD, cols)

        @pl.when(p < panel)
        def _():
            pltpu.make_async_copy(a_ref.at[p, upper], out.at[q, 0, upper], sem.at[2]).start()
            pltpu.make_async_copy(a_ref.at[p, lower], out.at[behind, 0, lower], sem.at[2]).start()

        return carry

    def fill_b(q, carry):
        p = b_pick[q]

        @pl.when(p < panel)
        def _():
            pltpu.make_async_copy(b_ref.at[p], out.at[q, 1], sem.at[3]).start()

        return carry

    load_a.wait()
    lax.fori_loop(0, a_pick.shape[0], fill_a, 0)
    load_b.wait()
    lax.fori_loop(0, b_pick.shape[0], fill_b, 0)
    pltpu.make_async_copy(a_blocks, a_ref, sem.at[2]).wait()
    pltpu.make_async_copy(b_blocks, b_ref, sem.at[3]).wait()


def fill(cols, a_pick, b_pick, small, a_blocks, b_blocks):
    slots = a_pick.shape[0]
    panel, width, _ = a_blocks.shape
    return pl.pallas_call(
        functools.partial(fill_kernel, cols),
        out_shape=jax.ShapeDtypeStruct((slots, 2, width, width), jnp.float32),
        in_specs=[SMEM] * 6 + [HBM, HBM],
        out_specs=HBM,
        scratch_shapes=[
            pltpu.VMEM((panel, width, width), jnp.float32),
            pltpu.VMEM((panel, width, width), jnp.float32),
            pltpu.SemaphoreType.DMA((4,)),
        ],
        compiler_params=pltpu.CompilerParams(vmem_limit_bytes=VMEM_LIMIT),
        cost_estimate=pl.CostEstimate(flops=0, bytes_accessed=16 * a_blocks.size, transcendentals=0),
        name="fill",
    )(a_pick, b_pick, *small, a_blocks, b_blocks)


def compact_kernel(parts, *refs):
    number = len(parts)
    places, arrived, outs, held = refs[:number], refs[number], refs[number + 1 : 2 * number + 1], refs[2 * number + 1 :]
    in_sem, out_sem = held[number:]
    pieces = [(n, k) for n in range(number) for k in range(PIECES)]
    for n, k in pieces:
        side, first, size = parts[n]
        step = places[n].shape[0] // PIECES

        def body(j, carry, n=n, k=k, side=side, rows=pl.ds(first, size)):
            source = arrived.at[places[n][j], side, rows]
            pltpu.make_async_copy(source, held[n].at[j], in_sem.at[n, k]).start()
            return carry

        lax.fori_loop(k * step, (k + 1) * step, body, 0, unroll=2)
    copies = []
    for n, k in pieces:
        step = places[n].shape[0] // PIECES
        piece = held[n].at[pl.ds(k * step, step)]
        copies.append(pltpu.make_async_copy(piece, outs[n].at[pl.ds(k * step, step)], out_sem.at[n, k]))
        pltpu.make_async_copy(piece, piece, in_sem.at[n, k]).wait()
        copies[-1].start()
    for copy in copies:
        copy.wait()


def compact(places, parts, arrived):
    width = arrived.shape[-1]
    shapes = [(place.shape[0], size, width) for place, (_, _, size) in zip(places, parts)]
    return pl.pallas_call(
        functools.partial(compact_kernel, tuple(parts)),
        out_shape=[jax.ShapeDtypeStruct(shape, jnp.float32) for shape in shapes],
        in_specs=[SMEM] * len(parts) + [HBM],
        out_specs=[HBM] * len(parts),
        scratch_shapes=[pltpu.VMEM(shape, jnp.float32) for shape in shapes]
        + [pltpu.SemaphoreType.DMA((len(parts), PIECES)), pltpu.SemaphoreType.DMA((len(parts), PIECES))],
        compiler_params=pltpu.CompilerParams(vmem_limit_bytes=VMEM_LIMIT),
        cost_estimate=pl.CostEstimate(flops=10**11, bytes_accessed=16 * 2**20, transcendentals=0),
        name="compact",
    )(*places, arrived)


def split(value):
    high = value.astype(jnp.bfloat16)
    low = (value - high.astype(jnp.float32)).astype(jnp.bfloat16)
    return high, low


def block_product(left, right):
    lh, ll = split(left)
    rh, rl = split(right)
    width = right.shape[1]
    wide = jnp.dot(
        jnp.concatenate([lh, ll], axis=1),
        jnp.concatenate(
            [jnp.concatenate([rh, rl], axis=1), jnp.concatenate([rh, jnp.zeros_like(rl)], axis=1)], axis=0
        ),
        preferred_element_type=jnp.float32,
    )
    return wide[:, :width] + wide[:, width:]


def add_all(c_ref, product, count):
    start = 0
    for group in GROUPS:

        def several(g, carry, group=group, start=start):
            for m, value in [product(start + g * group + u) for u in range(group)]:
                c_ref[m] += value
            return carry

        number = (count - start) // group
        lax.fori_loop(0, number, several, 0)
        start = start + number * group


def rows_of(ref, spec):
    if spec is None:
        return ref
    if len(spec) == 3:
        return ref.at[spec[0], pl.ds(spec[1], spec[2])]
    return ref.at[pl.ds(spec[0], spec[1])]


def products_kernel(jobs, has_c, flags, index_a, index_b, index_c, *refs):
    refs, scratch = refs[: len(refs) - len(jobs) * 2 - 3], refs[len(refs) - len(jobs) * 2 - 3 :]
    held = [(scratch[2 * n], scratch[2 * n + 1]) for n in range(len(jobs))]
    c_ref, live, sem = scratch[2 * len(jobs) :]
    c_out = refs[-1]
    blocks = c_out.shape[0]
    entries = index_a.shape[1]
    half = c_ref.shape[1] // 2

    if has_c:
        load_c = pltpu.make_async_copy(refs[-2], c_ref, sem.at[len(jobs), 0])
        load_c.start()
    waits = []
    for n, (_, _, _, upper, lower, b) in enumerate(jobs):
        a_ref, b_ref = held[n]
        copies = [
            pltpu.make_async_copy(rows_of(refs[upper[0]], upper[1]), a_ref.at[:, pl.ds(0, half)], sem.at[n, 0]),
            pltpu.make_async_copy(rows_of(refs[lower[0]], lower[1]), a_ref.at[:, pl.ds(half, half)], sem.at[n, 1]),
        ]
        for copy in copies:
            copy.start()
        for k, source in enumerate(b):
            copy = pltpu.make_async_copy(refs[source], b_ref, sem.at[n, 2])
            if len(b) == 1:
                copy.start()
            else:
                pl.when(flags[0] == k)(copy.start)
        waits.append([*copies, copy])

    counts = []
    for n, (t, first, size, _, _, _) in enumerate(jobs):

        def listing(e, count, n=n, t=t, first=first, size=size):
            live[n, count] = e
            slot = index_a[t, e]
            used = (index_c[t, e] < blocks) & (slot >= first) & (slot < first + size)
            return count + jnp.where(used, 1, 0)

        counts.append(lax.fori_loop(0, entries, listing, 0, unroll=4))
    if has_c:
        load_c.wait()
    else:
        c_ref[...] = jnp.zeros_like(c_ref)

    for n, (t, first, _, _, _, _) in enumerate(jobs):
        a_ref, b_ref = held[n]
        for copy in waits[n]:
            copy.wait()

        def product(at, n=n, t=t, first=first, a_ref=a_ref, b_ref=b_ref):
            e = live[n, at]
            return index_c[t, e], block_product(a_ref[index_a[t, e] - first], b_ref[index_b[t, e]])

        add_all(c_ref, product, counts[n])
    out = pltpu.make_async_copy(c_ref, c_out, sem.at[len(jobs), 0])
    out.start()
    out.wait()


def products(flags, prods, jobs, total):
    entries = prods[0].shape[1]
    width = jobs[0][5][0].shape[1]
    has_c = total is not None
    arrays = []

    def number(array):
        for n, known in enumerate(arrays):
            if known is array:
                return n
        arrays.append(array)
        return len(arrays) - 1

    static = []
    scratch = []
    for t, first, size, upper, lower, b in jobs:
        static.append((t, first, size, (number(upper[0]), upper[1]), (number(lower[0]), lower[1]), tuple(number(x) for x in b)))
        scratch.append(pltpu.VMEM((size, width, width), jnp.float32))
        scratch.append(pltpu.VMEM(b[0].shape, jnp.float32))
    operands = [flags, *prods, *arrays]
    aliases = {}
    if has_c:
        aliases = {len(operands): 0}
        operands.append(total)
    return pl.pallas_call(
        functools.partial(products_kernel, tuple(static), has_c),
        out_shape=jax.ShapeDtypeStruct((CBLK, width, width), jnp.float32),
        in_specs=[SMEM] * 4 + [ANY] * (len(operands) - 4),
        out_specs=ANY,
        scratch_shapes=scratch
        + [
            pltpu.VMEM((CBLK, width, width), jnp.float32),
            pltpu.SMEM((len(jobs), entries + 1), jnp.int32),
            pltpu.SemaphoreType.DMA((len(jobs) + 1, 3)),
        ],
        input_output_aliases=aliases,
        compiler_params=pltpu.CompilerParams(vmem_limit_bytes=VMEM_LIMIT),
        cost_estimate=pl.CostEstimate(
            flops=6000 * entries * width**3, bytes_accessed=8 * CBLK * width * width, transcendentals=0
        ),
        name="products",
    )(*operands)


def plan_kernel(ranges, index_a, index_b, index_c, plan):
    blocks = CBLK
    entries = index_a.shape[1]

    def clear(m, carry):
        plan[4, m] = -1
        return carry

    lax.fori_loop(0, blocks, clear, 0, unroll=8)
    counts = (0, 0)
    for n, (t, first, size) in enumerate(ranges):

        def note(e, counts, t=t, first=first, size=size):
            slot, m = index_a[t, e] - first, index_c[t, e]
            used = (m < blocks) & (slot >= 0) & (slot < size)
            count, kept = counts
            new = used & (plan[4, jnp.minimum(m, blocks - 1)] < 0)

            @pl.when(new)
            def _():
                plan[4, m] = kept
                plan[3, kept] = m

            @pl.when(used)
            def _():
                plan[0, count] = slot
                plan[1, count] = index_b[t, e]
                plan[2, count] = plan[4, m]

            return count + jnp.where(used, 1, 0), kept + jnp.where(new, 1, 0)

        counts = lax.fori_loop(0, entries, note, counts)
        plan[5, n] = counts[0]
    plan[5, len(ranges)] = counts[1]


def make_plan(prods, ranges):
    entries = prods[0].shape[1]
    return pl.pallas_call(
        functools.partial(plan_kernel, tuple(ranges)),
        out_shape=jax.ShapeDtypeStruct((6, max(len(ranges) * entries, CBLK)), jnp.int32),
        in_specs=[SMEM] * 3,
        out_specs=SMEM,
        name="plan",
    )(*prods)


def last_kernel(jobs, flags, plan, *refs):
    number = len(jobs)
    c_in, c_out, b_ref, c_ref, sem = refs[len(refs) - number - 5 : len(refs) - number - 3] + refs[len(refs) - 3 :]
    held = refs[len(refs) - number - 3 : len(refs) - 3]
    half = c_ref.shape[1] // 2
    kept = plan[5, number]

    copies = []
    for n, (upper, lower, _) in enumerate(jobs):
        for part, (source, spec) in enumerate((upper, lower)):
            rows = held[n].at[:, pl.ds(part * half, half)]
            copies.append(pltpu.make_async_copy(rows_of(refs[source], spec), rows, sem.at[2 + 2 * n + part]))
    for copy in copies:
        copy.start()

    begin = 0
    for n, (_, _, b) in enumerate(jobs):
        end = plan[5, n]

        def fetch(at, carry, b=b):
            for k, source in enumerate(b):
                copy = pltpu.make_async_copy(refs[source].at[plan[1, at]], b_ref.at[at], sem.at[0])
                if len(b) == 1:
                    copy.start()
                else:
                    pl.when(flags[0] == k)(copy.start)
            return carry

        lax.fori_loop(begin, end, fetch, 0)
        begin = end

    def fetch_c(k, carry):
        pltpu.make_async_copy(c_in.at[plan[3, k]], c_ref.at[k], sem.at[0]).start()
        return carry

    lax.fori_loop(0, kept, fetch_c, 0)

    def arrive(_, carry):
        pltpu.make_async_copy(c_in.at[0], c_ref.at[0], sem.at[0]).wait()
        return carry

    lax.fori_loop(0, begin + kept, arrive, 0)
    for copy in copies:
        copy.wait()

    begin = 0
    for n in range(number):
        end = plan[5, n]

        def product(at, a_ref=held[n]):
            return plan[2, at], block_product(a_ref[plan[0, at]], b_ref[at])

        add_all(c_ref, lambda at, begin=begin, product=product: product(begin + at), end - begin)
        begin = end

    def store(k, carry):
        pltpu.make_async_copy(c_ref.at[k], c_out.at[plan[3, k]], sem.at[1]).start()
        return carry

    lax.fori_loop(0, kept, store, 0)

    def leave(_, carry):
        pltpu.make_async_copy(c_ref.at[0], c_out.at[0], sem.at[1]).wait()
        return carry

    lax.fori_loop(0, kept, leave, 0)


def last_products(flags, plan, entries, jobs, total):
    block = total.shape[1:]
    arrays = []
    static = []
    for _, _, size, upper, lower, b in jobs:
        n = len(arrays)
        arrays += [upper[0], lower[0], *b]
        static.append(((n, upper[1]), (n + 1, lower[1]), tuple(range(n + 2, len(arrays)))))
    operands = [flags, plan, *arrays, total]
    return pl.pallas_call(
        functools.partial(last_kernel, tuple(static)),
        out_shape=jax.ShapeDtypeStruct(total.shape, jnp.float32),
        in_specs=[SMEM] * 2 + [ANY] * (len(operands) - 2),
        out_specs=ANY,
        scratch_shapes=[pltpu.VMEM((size, *block), jnp.float32) for _, _, size, _, _, _ in jobs]
        + [
            pltpu.VMEM((len(jobs) * entries, *block), jnp.float32),
            pltpu.VMEM(total.shape, jnp.float32),
            pltpu.SemaphoreType.DMA((2 + 2 * len(jobs),)),
        ],
        input_output_aliases={len(operands) - 1: 0},
        compiler_params=pltpu.CompilerParams(vmem_limit_bytes=VMEM_LIMIT),
        cost_estimate=pl.CostEstimate(
            flops=6000 * entries * block[0] ** 3, bytes_accessed=8 * total.size, transcendentals=0
        ),
        name="last_products",
    )(*operands)


def together(*values):
    return lax.optimization_barrier(values)


def local(a_blocks, a_pick, a_place, b_blocks, b_pick, b_place, prod_a, prod_b, prod_c):
    flags = jnp.stack([lax.axis_index("row") % 2, lax.axis_index("col") % 2]).astype(jnp.int32)
    prods = (prod_a, prod_b, prod_c)
    outgoing = fill(lax.axis_size("col"), a_pick, b_pick, (*prods, flags), a_blocks, b_blocks)
    outgoing, flags = together(outgoing, flags)
    arrived = lax.all_to_all(outgoing, ("row", "col"), split_axis=0, concat_axis=0, tiled=True)
    width = arrived.shape[-1]
    half = width // 2
    arrived, a_place = together(arrived, a_place)
    far_place = permute(a_place, lambda r, c: (r, c + AHEAD))
    (b0,) = compact([b_place], [(1, 0, width)], arrived)
    arrived, b0 = together(arrived, b0)
    (up0,) = compact([a_place], [(0, 0, half)], arrived)
    arrived, far_place, up0 = together(arrived, far_place, up0)
    (low3,) = compact([far_place], [(0, half, half)], arrived)
    up0, low3, flags = together(up0, low3, flags)
    core1, odd = flags[0] == 1, flags[1] == 1

    up2 = permute(up0, lambda r, c: (r, c + 2))
    low1 = permute(low3, lambda r, c: (r, c - 2))
    b2 = permute(b0, lambda r, c: (r + 2, c))
    near0 = permute(b0, lambda r, c: (r ^ 1, c))
    firsts = [sum(SIZES[:i]) for i in range(len(SIZES))]
    last = len(SIZES) - 1
    cross = []
    for first, size in zip(firsts, SIZES):
        rows = slice(first, first + size)
        cross.append((jnp.where(odd, up0[rows], up2[rows]), jnp.where(odd, low1[rows], low3[rows])))
    cross = [jnp.stack(pair) for pair in cross[:last]] + [*cross[last]]
    plan = make_plan(prods, [(t, firsts[last], SIZES[last]) for t in (0, 3)])
    *cross, b0, b2, near0, plan = together(*cross, b0, b2, near0, plan)

    def over(part):
        return permute(part, lambda r, c: (r, c ^ 1))

    mid = [over(part) for part in cross[:last]]
    cross[last], cross[last + 1], mid[0] = together(cross[last], cross[last + 1], mid[0])
    mid += [over(cross[last]), over(cross[last + 1])]
    near2 = permute(b2, lambda r, c: (r ^ 1, c))
    far3 = permute(b0, lambda r, c: (r + 3, c) if r % 2 else None)
    b1, b3 = [near0, near2], [near2, far3]
    ends = []

    def onward(up1, low2):
        up3 = permute(up1, lambda r, c: (r, c + 2))
        low0 = permute(low2, lambda r, c: (r, c - 2))
        ends.append((up3, low0))

    def middle(i, up1, low2):
        first, size = firsts[i], SIZES[i]
        part = (first, size)
        return [(1, first, size, up1, (low1, part), b1), (2, first, size, (up2, part), low2, [b2])]

    def outer(i):
        first, size = firsts[i], SIZES[i]
        part = (first, size)
        return [
            (0, first, size, (up0, part), (ends[i][1], None), [b0]),
            (3, first, size, (ends[i][0], None), (low3, part), b3),
        ]

    total = None
    jobs = []
    for i in range(last):
        if i > 0:
            mid[i], total = together(mid[i], total)
        onward(mid[i][0], mid[i][1])
        size = SIZES[i]
        jobs = middle(i, (mid[i], (0, 0, size)), (mid[i], (1, 0, size))) + jobs
        total = products(flags, prods, jobs, total)
        jobs = outer(i)
    mid[last], mid[last + 1], total = together(mid[last], mid[last + 1], total)
    onward(mid[last], mid[last + 1])
    jobs = middle(last, (mid[last], None), (mid[last + 1], None)) + jobs
    total = products(flags, prods, jobs, total)
    return last_products(flags, plan, prod_a.shape[1], outer(last), total)


def solution(mesh):
    placed = (
        P(("row", "col"), None, None),
        P(("row", "col")),
        P(("row", "col")),
        P(("row", "col"), None, None),
        P(("row", "col")),
        P(("row", "col")),
        P(None, ("row", "col")),
        P(None, ("row", "col")),
        P(None, ("row", "col")),
    )
    return jax.shard_map(
        local, mesh=mesh, in_specs=placed, out_specs=P(("row", "col"), None, None), check_vma=False
    )
```
